256 devices in a mesh: tile: 32 (over y, x, z_hi), lev: 8 (over z_lo, core).
Axes of the slice: x: 4, y: 4, z: 8 (z_hi: 2, z_lo: 4; z = z_hi * 4 + z_lo), core: 2. Of those that a mesh axis runs over, the one named last changes fastest.
Arguments:
- thickness: float32 [16, 256, 1024], P('lev', 'tile'), may hold values from 1 to 3
- wind_east: float32 [16, 256, 1024], P('lev', 'tile'), may hold values from -4 to 4
- wind_north: float32 [16, 256, 1024], P('lev', 'tile'), may hold values from -4 to 4
- theta: float32 [16, 256, 1024], P('lev', 'tile'), may hold values from 0.5 to 1.5
- tracer: float32 [16, 256, 1024], P('lev', 'tile'), may hold values from 0 to 1
- wind_vertical: float32 [16, 256, 1024], P('lev', 'tile'), may hold values from -2 to 2
- cross_index: int32 [15, 256, 1024], P(None, 'tile', 'lev'), may hold values from 0 to 15, as said below
- cross_slot: int32 [15, 256, 1024], P(None, 'tile', 'lev'), may hold values from 0 to 7, as said below
Outputs:
- remapped_thickness: float32 [16, 256, 1024], P(None, 'tile', 'lev')
- remapped_east: float32 [16, 256, 1024], P(None, 'tile', 'lev')
- remapped_north: float32 [16, 256, 1024], P(None, 'tile', 'lev')
- remapped_theta: float32 [16, 256, 1024], P(None, 'tile', 'lev')
- remapped_tracer: float32 [16, 256, 1024], P(None, 'tile', 'lev')
- remapped_vertical: float32 [16, 256, 1024], P(None, 'tile', 'lev')
The draws below stay inside these ranges and needn't reach their ends.
Inputs may be any that keep to these rules, and one draw needn't show every extreme that they name: For each column the positions cross_index * 8 + cross_slot of interfaces j = 1 to 15 lie within 3 slots of j * 8, so they increase with j by 2 to 14 slots. `cross_slot`: slot within the layer named by cross_index, as described there.
All inputs are finite; a program needn't handle non-finite values.
Results may differ from the reference program's by a relative error of at most 0.000022.
Values sent between devices are 32-bit elements; how exact they have to be, the bound alone decides.
A program may use at most 64 MiB of HBM per device.

```python
import jax
import jax.numpy as jnp
from jax import lax

SUBSTEPS = 3
SLOTS = 8
NLEV = 16
NX = 256
NY = 1024


def target_slots(key):
    offsets = jax.random.randint(key, (NLEV - 1, NX, NY), -(SLOTS // 2 - 1), SLOTS // 2, dtype=jnp.int32)
    centres = (jnp.arange(1, NLEV, dtype=jnp.int32) * SLOTS)[:, None, None]
    return centres + offsets


def draw_cross_index(key, part):
    slots = target_slots(key)
    return (slots // SLOTS).astype(jnp.int32)


def draw_cross_slot(key, part):
    slots = target_slots(key)
    return (slots % SLOTS).astype(jnp.int32)


def levels(own_key, shape, shards, smallest, largest):
    def one(dim, parts):
        heights = jax.random.uniform(jax.random.fold_in(jax.random.fold_in(own_key, 6), dim), (parts,), jnp.float32, smallest / len(shards), largest / len(shards))
        return jnp.repeat(jnp.exp(heights), shape[dim] // parts).reshape((-1,) + (1,) * (len(shape) - dim - 1))

    level = one(*shards[0])
    for cut in shards[1:]:
        level = level * one(*cut)
    return level


def normal_values(rng, dims, width, most, pieces=(), kind=jnp.bfloat16):
    result = width * jax.random.normal(rng, dims, jnp.float32)
    if pieces:
        result = result * levels(rng, dims, pieces, -0.22, 0.18)
    return jnp.clip(result, -most, most).astype(kind)


def setup_inputs(seed: int = 0) -> dict:
    arg_keys = jax.random.split(jax.random.key(seed), 9)
    return {
        "thickness": jnp.clip(1.0 + 2.0 * jax.random.uniform(arg_keys[0], (NLEV, NX, NY), jnp.float32) ** levels(arg_keys[0], (NLEV, NX, NY), ((0, 8), (1, 32)), -0.2, 0.2), 1.0, 3.0),
        "wind_east": normal_values(arg_keys[1], (NLEV, NX, NY), 1.0, 4.0, ((0, 8), (1, 32)), jnp.float32),
        "wind_north": normal_values(arg_keys[2], (NLEV, NX, NY), 1.0, 4.0, ((0, 8), (1, 32)), jnp.float32),
        "theta": jnp.clip(0.5 + 1.0 * jax.random.uniform(arg_keys[3], (NLEV, NX, NY), jnp.float32) ** levels(arg_keys[3], (NLEV, NX, NY), ((0, 8), (1, 32)), -0.2, 0.2), 0.5, 1.5),
        "tracer": jnp.clip(1.0 * jax.random.uniform(arg_keys[4], (NLEV, NX, NY), jnp.float32) ** levels(arg_keys[4], (NLEV, NX, NY), ((0, 8), (1, 32)), -0.2, 0.2), 0.0, 1.0),
        "wind_vertical": normal_values(arg_keys[5], (NLEV, NX, NY), 0.5, 2.0, ((0, 8), (1, 32)), jnp.float32),
        "cross_index": draw_cross_index(jax.random.fold_in(arg_keys[8], 71), 0),
        "cross_slot": draw_cross_slot(jax.random.fold_in(arg_keys[8], 71), 0),
    }


courant = 0.1
damping = 0.015


def shifted(field, offset, axis):
    return jnp.roll(field, -offset, axis)


def slope(field, axis):
    return (45.0 * (shifted(field, 1, axis) - shifted(field, -1, axis)) - 9.0 * (shifted(field, 2, axis) - shifted(field, -2, axis)) + (shifted(field, 3, axis) - shifted(field, -3, axis))) / 60.0


def sixth(field, axis):
    return (shifted(field, 3, axis) + shifted(field, -3, axis)) - 6.0 * (shifted(field, 2, axis) + shifted(field, -2, axis)) + 15.0 * (shifted(field, 1, axis) + shifted(field, -1, axis)) - 20.0 * field


def substep(state):
    logthick, east, north, temper, mixing, upward = state
    fields = (logthick, east, north, temper, mixing, upward)
    slope_x = [slope(f, 0) for f in fields]
    slope_y = [slope(f, 1) for f in fields]
    damps = [damping * (sixth(f, 0) + sixth(f, 1)) for f in fields]
    divergence = slope_x[1] + slope_y[2]

    def carried(which):
        return east * slope_x[which] + north * slope_y[which]

    new_log = logthick - courant * (divergence + carried(0)) + damps[0]
    pressure = temper * jnp.exp(new_log)
    new_east = east - courant * (slope(pressure, 0) + carried(1)) + damps[1]
    new_north = north - courant * (slope(pressure, 1) + carried(2)) + damps[2]
    new_temper = temper - courant * carried(3) + damps[3]
    new_mixing = mixing - courant * carried(4) + damps[4]
    new_upward = upward - courant * (carried(5) + divergence) + damps[5]
    return (new_log, new_east, new_north, new_temper, new_mixing, new_upward)


def advance_level(state):
    for step in range(SUBSTEPS):
        state = substep(state)
    return state


def layer_edges(field):
    inner = (7.0 * (field[1:-2] + field[2:-1]) - (field[:-3] + field[3:])) / 12.0
    return jnp.concatenate([field[:1], 0.5 * (field[:1] + field[1:2]), inner, 0.5 * (field[-2:-1] + field[-1:]), field[-1:]], axis=0)


def running_before(weights):
    running = jnp.cumsum(weights, axis=0)
    before = jnp.concatenate([jnp.zeros_like(weights[:1]), running[:-1]], axis=0)
    return before, running[-1:]


def remap_all(thick, fields, layer_index, fraction):
    thick_at = jnp.take_along_axis(thick, layer_index, axis=0)
    mass_before, mass_total = running_before(thick)
    mass_cross = jnp.take_along_axis(mass_before, layer_index, axis=0) + fraction * thick_at
    mass_full = jnp.concatenate([jnp.zeros_like(mass_total), mass_cross, mass_total], axis=0)
    thickness_out = mass_full[1:] - mass_full[:-1]
    results = [thickness_out]
    square = 0.5 * fraction * fraction
    cubic = fraction * fraction * fraction / 3.0
    for field in fields:
        edges = layer_edges(field)
        left = edges[:-1]
        right = edges[1:]
        curve = 6.0 * field - 3.0 * (left + right)
        left_at = jnp.take_along_axis(left, layer_index, axis=0)
        right_at = jnp.take_along_axis(right, layer_index, axis=0)
        curve_at = jnp.take_along_axis(curve, layer_index, axis=0)
        partial_part = fraction * left_at + square * (right_at - left_at) + curve_at * (square - cubic)
        content_before, content_total = running_before(thick * field)
        cross = jnp.take_along_axis(content_before, layer_index, axis=0) + thick_at * partial_part
        full = jnp.concatenate([jnp.zeros_like(content_total), cross, content_total], axis=0)
        results.append((full[1:] - full[:-1]) / thickness_out)
    return results


def reference(thickness, wind_east, wind_north, theta, tracer, wind_vertical, cross_index, cross_slot):
    state = (jnp.log(thickness), wind_east, wind_north, theta, tracer, wind_vertical)
    state = lax.map(advance_level, state)
    thick = jnp.exp(state[0])
    fraction = cross_slot.astype(jnp.float32) / SLOTS
    results = remap_all(thick, list(state[1:]), cross_index.astype(jnp.int32), fraction)
    return (results[0], results[1], results[2], results[3], results[4], results[5])
```

```python
import functools

import jax
import jax.numpy as jnp
from jax import lax
from jax.experimental import pallas as pl
from jax.experimental.pallas import tpu as pltpu
from jax.sharding import PartitionSpec as P

MESH = pl.DeviceIdType.MESH

COURANT = 0.1
DAMPING = 0.015
SLOPE = (45.0 / 60.0, -9.0 / 60.0, 1.0 / 60.0)
SIXTH = (15.0, -6.0, 1.0)
SLOTS = 8

LANES = 128
SUB = 8
PIECES = 8
LEVELS = 16
FIELDS = 6
COLUMNS = 16
OFF = 24
ROWS = 64

REACH = (((0, 16), (0, 16)), ((0, 16), (0, 16)), ((1, 15), (0, 15)), ((1, 15), (0, 15)), ((7, 9), (0, 9)), ((7, 9), (0, 9)))


def place():
    tile = lax.axis_index("tile")
    lev = lax.axis_index("lev")
    high = lax.rem(tile, 2)
    column = lax.div(tile, 2)
    ring = high * 4 + lax.div(lev, 2)
    core = lax.rem(lev, 2)
    return column, ring, core


def device(column, ring, core):
    column = lax.rem(column + 2 * COLUMNS, COLUMNS)
    ring = lax.rem(ring + 16, 8)
    return (column * 2 + lax.div(ring, 4), lax.rem(ring, 4) * 2 + core)


def owned_level(ring, core):
    first = jnp.logical_and(ring >= 2, ring < 6)
    early = 4 * (ring - 2) + 2 * core
    late = 4 * lax.rem(ring + 2, 8) + 2 * core + 1
    return jnp.where(first, early, late)


def lanes():
    return lax.broadcasted_iota(jnp.int32, (SUB, LANES), 1)


def shifted_y(get, piece, row, lane):
    before = lax.rem(piece + PIECES - 1, PIECES)
    after = lax.rem(piece + 1, PIECES)
    here, left, right = get(piece, row), get(before, row), get(after, row)
    ahead, behind = [], []
    for k in (1, 2, 3):
        ahead.append(pltpu.roll(jnp.where(lane < k, right, here), LANES - k, 1))
        behind.append(pltpu.roll(jnp.where(lane >= LANES - k, left, here), k, 1))
    return here, ahead, behind


def shifted_x(get, piece, row):
    return [get(piece, row + k) for k in (1, 2, 3)], [get(piece, row - k) for k in (1, 2, 3)]


def slope(ahead, behind):
    total = None
    for k in range(3):
        term = (-COURANT * SLOPE[k]) * (ahead[k] - behind[k])
        total = term if total is None else total + term
    return total


def weights(wind):
    plus, minus = [], []
    for k in range(3):
        carry = wind * (-COURANT * SLOPE[k])
        plus.append(DAMPING * SIXTH[k] + carry)
        minus.append(DAMPING * SIXTH[k] - carry)
    return plus, minus


def stencil(here, x_side, y_side, by_x, by_y):
    total = (1.0 - 40.0 * DAMPING) * here
    for (ahead, behind), (plus, minus) in ((x_side, by_x), (y_side, by_y)):
        for k in range(3):
            total = total + plus[k] * ahead[k]
            total = total + minus[k] * behind[k]
    return total


def reader(ref, field):
    def get(piece, row):
        return ref[field, piece, pl.ds(OFF + row, SUB), :]

    return get


def mass_stage(log_get, old, pressure, divergence, step, start, blocks, store):
    def run(piece, carry):
        lane = lanes()
        for block in range(blocks):
            row = start + SUB * block
            east = reader(old, 1)
            north = reader(old, 2)
            by_x = weights(east(piece, row))
            n_here, n_ahead, n_behind = shifted_y(north, piece, row, lane)
            by_y = weights(n_here)
            div = slope(*shifted_x(east, piece, row)) + slope(n_ahead, n_behind)
            g_here, g_ahead, g_behind = shifted_y(log_get, piece, row, lane)
            new = stencil(g_here, shifted_x(log_get, piece, row), (g_ahead, g_behind), by_x, by_y) + div
            thick = jnp.exp(new)
            at = pl.ds(OFF + row, SUB)
            divergence[step, piece, at, :] = div
            pressure[step, piece, at, :] = reader(old, 3)(piece, row) * thick
            store(piece, row, new, thick)
        return carry

    lax.fori_loop(0, PIECES, run, 0)


def wind_piece(old, pressure, step, piece, row, lane):
    east, north, temper, press = reader(old, 1), reader(old, 2), reader(old, 3), reader(pressure, step)
    e_here, e_ahead, e_behind = shifted_y(east, piece, row, lane)
    n_here, n_ahead, n_behind = shifted_y(north, piece, row, lane)
    by_x, by_y = weights(e_here), weights(n_here)
    new_east = stencil(e_here, shifted_x(east, piece, row), (e_ahead, e_behind), by_x, by_y)
    new_east = new_east + slope(*shifted_x(press, piece, row))
    new_north = stencil(n_here, shifted_x(north, piece, row), (n_ahead, n_behind), by_x, by_y)
    _, p_ahead, p_behind = shifted_y(press, piece, row, lane)
    new_north = new_north + slope(p_ahead, p_behind)
    t_here, t_ahead, t_behind = shifted_y(temper, piece, row, lane)
    new_temper = stencil(t_here, shifted_x(temper, piece, row), (t_ahead, t_behind), by_x, by_y)
    return new_east, new_north, new_temper


def passive_piece(old, divergence, step, piece, row, lane):
    by_x = weights(reader(old, 1)(piece, row))
    by_y = weights(reader(old, 2)(piece, row))
    out = []
    for field in (4, 5):
        get = reader(old, field)
        here, ahead, behind = shifted_y(get, piece, row, lane)
        out.append(stencil(here, shifted_x(get, piece, row), (ahead, behind), by_x, by_y))
    out[1] = out[1] + divergence[step, piece, pl.ds(OFF + row, SUB), :]
    return out


def stage(body, start, blocks, store):
    def run(piece, carry):
        lane = lanes()
        for block in range(blocks):
            row = start + SUB * block
            store(piece, row, body(piece, row, lane))
        return carry

    lax.fori_loop(0, PIECES, run, 0)


def advance_kernel(*refs):
    inputs = refs[:FIELDS]
    got_a, got_b = refs[FIELDS : FIELDS + 2]
    (state0, state1, state2, logs, pressure, divergence, out_a, out_b, z_send, z_recv, x_send, x_recv, far_send, far_recv, all_send, all_recv, own_sem) = refs[FIELDS + 2 :]

    column, ring, core = place()
    high = lax.div(ring, 4)

    barrier = pltpu.get_barrier_semaphore()
    partners = [device(column + d, ring, core) for d in (1, -1, 2, -2)]
    partners += [device(column, ring + d, lax.rem(core + c, 2)) for d in (4, 3, 5, 2, 6, 1, 7, 0) for c in (0, 1) if d or c]
    for who in partners:
        pl.semaphore_signal(barrier, inc=1, device_id=who, device_id_type=MESH)
    pl.semaphore_wait(barrier, len(partners))

    half = pl.ds(pl.multiple_of(OFF + SUB * high, SUB), SUB)
    sends = []
    z_copies = []
    for field in range(FIELDS):
        pair = []
        for way, (level, hop) in enumerate(((high, 2), (1 - high, -2))):
            copy = pltpu.make_async_remote_copy(
                src_ref=inputs[field].at[level],
                dst_ref=state0.at[field, :, half, :],
                send_sem=z_send.at[field, way],
                recv_sem=z_recv.at[field, way],
                device_id=device(column, ring + hop, core),
                device_id_type=MESH,
            )
            copy.start()
            pair.append(copy)
            sends.append(copy)
        z_copies.append(pair)

    x_copies = []
    for field in range(FIELDS):
        for copy in z_copies[field]:
            copy.wait_recv()
        group = []
        for way in (0, 1):
            first, count = REACH[field][way]
            shift = -16 if way == 0 else 16
            copy = pltpu.make_async_remote_copy(
                src_ref=state0.at[field, :, pl.ds(OFF + first, count), :],
                dst_ref=state0.at[field, :, pl.ds(OFF + first + shift, count), :],
                send_sem=x_send.at[field, way],
                recv_sem=x_recv.at[field, way],
                device_id=device(column + (1 if way == 0 else -1), ring, core),
                device_id_type=MESH,
            )
            copy.start()
            group.append(copy)
        if field < 2:
            for way in (0, 1):
                first, shift = (14, -32) if way == 0 else (0, 32)
                copy = pltpu.make_async_remote_copy(
                    src_ref=state0.at[field, :, pl.ds(OFF + first, 2), :],
                    dst_ref=state0.at[field, :, pl.ds(OFF + first + shift, 2), :],
                    send_sem=far_send.at[field, way],
                    recv_sem=far_recv.at[field, way],
                    device_id=device(column + (2 if way == 0 else -2), ring, core),
                    device_id_type=MESH,
                )
                copy.start()
                group.append(copy)
        x_copies.append(group)
        sends += group

    for copy in x_copies[0]:
        copy.wait_recv()

    def take_log(piece, carry):
        for block in range(7):
            at = pl.ds(OFF - 18 + SUB * block, SUB)
            logs[0, piece, at, :] = jnp.log(state0[0, piece, at, :])
        return carry

    lax.fori_loop(0, PIECES, take_log, 0)

    for field in (1, 2, 3):
        for copy in x_copies[field]:
            copy.wait_recv()

    def keep(ref, fields):
        def store(piece, row, values):
            for field, value in zip(fields, values):
                ref[field, piece, pl.ds(OFF + row, SUB), :] = value

        return store

    def keep_log(ref):
        def store(piece, row, new, thick):
            ref[0, piece, pl.ds(OFF + row, SUB), :] = new

        return store

    def keep_thick(piece, row, new, thick):
        logs[0, piece, pl.ds(OFF + row, SUB), :] = thick

    states = (state0, state1, state2)
    mass_stage(reader(logs, 0), state0, pressure, divergence, 0, -16, 6, keep_log(state1))
    stage(functools.partial(wind_piece, state0, pressure, 0), -12, 5, keep(state1, (1, 2, 3)))
    mass_stage(reader(state1, 0), state1, pressure, divergence, 1, -12, 5, keep_log(state2))
    stage(functools.partial(wind_piece, state1, pressure, 1), -8, 4, keep(state2, (1, 2, 3)))
    mass_stage(reader(state2, 0), state2, pressure, divergence, 2, -4, 3, keep_thick)

    level = owned_level(ring, core)
    lev = lax.rem(ring, 4) * 2 + core

    def give(piece, part, out, got):
        for tile_half in (0, 1):
            mine = jnp.logical_and(piece == lev, high == tile_half)
            slot = piece * 2 + tile_half

            @pl.when(mine)
            def _():
                pltpu.make_async_copy(out.at[piece, tile_half], got.at[level], own_sem.at[part]).start()

            @pl.when(jnp.logical_not(mine))
            def _():
                pltpu.make_async_remote_copy(
                    src_ref=out.at[piece, tile_half],
                    dst_ref=got.at[level],
                    send_sem=all_send.at[part, slot],
                    recv_sem=all_recv.at[part, level],
                    device_id=(column * 2 + tile_half, piece),
                    device_id_type=MESH,
                ).start()

    def last_winds(turn, carry):
        piece = lax.rem(lax.rem(ring, 4) * 2 + turn, PIECES)
        lane = lanes()
        for tile_half in (0, 1):
            row = SUB * tile_half
            out_a[piece, tile_half, 0, :, :] = logs[0, piece, pl.ds(OFF + row, SUB), :]
            for n, value in enumerate(wind_piece(state2, pressure, 2, piece, row, lane)):
                out_a[piece, tile_half, n + 1, :, :] = value
        give(piece, 0, out_a, got_a)
        return carry

    lax.fori_loop(0, PIECES, last_winds, 0)

    for field in (4, 5):
        for copy in x_copies[field]:
            copy.wait_recv()

    stage(functools.partial(passive_piece, state0, divergence, 0), -8, 4, keep(state1, (4, 5)))
    stage(functools.partial(passive_piece, state1, divergence, 1), -4, 3, keep(state2, (4, 5)))

    def last_passive(turn, carry):
        piece = lax.rem(lax.rem(ring, 4) * 2 + turn, PIECES)
        lane = lanes()
        for tile_half in (0, 1):
            for n, value in enumerate(passive_piece(state2, divergence, 2, piece, SUB * tile_half, lane)):
                out_b[piece, tile_half, n, :, :] = value
        give(piece, 1, out_b, got_b)
        return carry

    lax.fori_loop(0, PIECES, last_passive, 0)

    for copy in sends:
        copy.wait_send()

    def finish(part, out, got):
        def run(slot, carry):
            @pl.when(slot != lev * 2 + high)
            def _():
                pltpu.make_async_copy(out.at[0, 0], out.at[0, 0], all_send.at[part, slot]).wait()

            @pl.when(slot != level)
            def _():
                pltpu.make_async_copy(got.at[slot], got.at[slot], all_recv.at[part, slot]).wait()

            return carry

        lax.fori_loop(0, LEVELS, run, 0)
        pltpu.make_async_copy(out.at[0, 0], got.at[0], own_sem.at[part]).wait()

    finish(0, out_a, got_a)
    finish(1, out_b, got_b)


def advance(fields):
    state = pltpu.VMEM((FIELDS, PIECES, ROWS, LANES), jnp.float32)
    return pl.pallas_call(
        advance_kernel,
        out_shape=(
            jax.ShapeDtypeStruct((LEVELS, 4, SUB, LANES), jnp.float32),
            jax.ShapeDtypeStruct((LEVELS, 2, SUB, LANES), jnp.float32),
        ),
        in_specs=[pl.BlockSpec(memory_space=pl.ANY)] * FIELDS,
        out_specs=(pl.BlockSpec(memory_space=pl.ANY), pl.BlockSpec(memory_space=pl.ANY)),
        scratch_shapes=[
            state,
            state,
            state,
            pltpu.VMEM((1, PIECES, ROWS, LANES), jnp.float32),
            pltpu.VMEM((3, PIECES, ROWS, LANES), jnp.float32),
            pltpu.VMEM((3, PIECES, ROWS, LANES), jnp.float32),
            pltpu.VMEM((PIECES, 2, 4, SUB, LANES), jnp.float32),
            pltpu.VMEM((PIECES, 2, 2, SUB, LANES), jnp.float32),
            pltpu.SemaphoreType.DMA((FIELDS, 2)),
            pltpu.SemaphoreType.DMA((FIELDS, 2)),
            pltpu.SemaphoreType.DMA((FIELDS, 2)),
            pltpu.SemaphoreType.DMA((FIELDS, 2)),
            pltpu.SemaphoreType.DMA((2, 2)),
            pltpu.SemaphoreType.DMA((2, 2)),
            pltpu.SemaphoreType.DMA((2, LEVELS)),
            pltpu.SemaphoreType.DMA((2, LEVELS)),
            pltpu.SemaphoreType.DMA((2,)),
        ],
        name="advance",
        compiler_params=pltpu.CompilerParams(
            collective_id=0, has_side_effects=True, vmem_limit_bytes=32 * 1024 * 1024
        ),
    )(*fields)


def remap_kernel(got_a, got_b, index_ref, slot_ref, *outs):
    thick = [got_a[k, 0] for k in range(LEVELS)]
    before = [jnp.zeros_like(thick[0])]
    for k in range(LEVELS):
        before.append(before[-1] + thick[k])
    picks, parts = [], []
    mass = [before[0]]
    for j in range(1, LEVELS):
        upper = index_ref[j - 1] == j
        x = slot_ref[j - 1].astype(jnp.float32) * (1.0 / SLOTS)
        square = 0.5 * x * x
        bend = square - x * x * x * (1.0 / 3.0)
        at = jnp.where(upper, thick[j], thick[j - 1])
        mass.append(jnp.where(upper, before[j], before[j - 1]) + x * at)
        picks.append(upper)
        parts.append((at, x - square - 3.0 * bend, square - 3.0 * bend, 6.0 * bend))
    mass.append(before[LEVELS])
    layer = []
    for j in range(LEVELS):
        layer.append(mass[j + 1] - mass[j])
        outs[0][j] = layer[j]
    for field in range(5):
        if field < 3:
            f = [got_a[k, field + 1] for k in range(LEVELS)]
        else:
            f = [got_b[k, field - 3] for k in range(LEVELS)]
        edge = [f[0], 0.5 * (f[0] + f[1])]
        for k in range(2, LEVELS - 1):
            edge.append((7.0 * (f[k - 1] + f[k]) - (f[k - 2] + f[k + 1])) * (1.0 / 12.0))
        edge += [0.5 * (f[-2] + f[-1]), f[-1]]
        running = jnp.zeros_like(f[0])
        sums = [running]
        for k in range(LEVELS):
            running = running + thick[k] * f[k]
            sums.append(running)
        last = sums[0]
        for j in range(1, LEVELS + 1):
            if j < LEVELS:
                upper = picks[j - 1]
                at, w_left, w_right, w_mid = parts[j - 1]
                left = jnp.where(upper, edge[j], edge[j - 1])
                right = jnp.where(upper, edge[j + 1], edge[j])
                mid = jnp.where(upper, f[j], f[j - 1])
                base = jnp.where(upper, sums[j], sums[j - 1])
                content = base + at * (w_left * left + w_right * right + w_mid * mid)
            else:
                content = sums[LEVELS]
            outs[field + 1][j - 1] = (content - last) / layer[j - 1]
            last = content


def remap(got_a, got_b, index, slot):
    vmem = pl.BlockSpec(memory_space=pltpu.VMEM)
    return pl.pallas_call(
        remap_kernel,
        out_shape=tuple(jax.ShapeDtypeStruct((LEVELS, SUB, LANES), jnp.float32) for _ in range(6)),
        in_specs=[vmem] * 4,
        out_specs=tuple([vmem] * 6),
        name="remap",
    )(got_a, got_b, index, slot)


def body(thickness, wind_east, wind_north, theta, tracer, wind_vertical, cross_index, cross_slot):
    fields = [
        f.reshape(2, SUB, PIECES, LANES).transpose(0, 2, 1, 3)
        for f in (thickness, wind_east, wind_north, theta, tracer, wind_vertical)
    ]
    got_a, got_b = advance(fields)
    return tuple(remap(got_a, got_b, cross_index, cross_slot))


def solution(mesh):
    split = P("lev", "tile", None)
    joined = P(None, "tile", "lev")
    return jax.shard_map(
        body,
        mesh=mesh,
        in_specs=(split,) * 6 + (joined,) * 2,
        out_specs=(joined,) * 6,
        check_vma=False,
    )
```

```python
import functools

import jax
import jax.numpy as jnp
from jax import lax
from jax.experimental import pallas as pl
from jax.experimental.pallas import tpu as pltpu
from jax.sharding import PartitionSpec as P

MESH = pl.DeviceIdType.MESH

COURANT = 0.1
DAMPING = 0.015
SLOPE = (45.0 / 60.0, -9.0 / 60.0, 1.0 / 60.0)
SIXTH = (15.0, -6.0, 1.0)
SLOTS = 8

LANES = 128
SUB = 8
PIECES = 8
LEVELS = 16
FIELDS = 6
COLUMNS = 16
OFF = 24
ROWS = 64
AHEAD = 2

REACH = (((0, 16), (0, 16)), ((0, 16), (0, 16)), ((1, 15), (0, 15)), ((1, 15), (0, 15)), ((7, 9), (0, 9)), ((7, 9), (0, 9)))


def place():
    tile = lax.axis_index("tile")
    lev = lax.axis_index("lev")
    high = lax.rem(tile, 2)
    column = lax.div(tile, 2)
    ring = high * 4 + lax.div(lev, 2)
    core = lax.rem(lev, 2)
    return column, ring, core


def device(column, ring, core):
    column = lax.rem(column + 2 * COLUMNS, COLUMNS)
    ring = lax.rem(ring + 16, 8)
    return (column * 2 + lax.div(ring, 4), lax.rem(ring, 4) * 2 + core)


def owned_level(ring, core):
    first = jnp.logical_and(ring >= 2, ring < 6)
    early = 4 * (ring - 2) + 2 * core
    late = 4 * lax.rem(ring + 2, 8) + 2 * core + 1
    return jnp.where(first, early, late)


def lanes():
    return lax.broadcasted_iota(jnp.int32, (SUB, LANES), 1)


def shifted_y(get, piece, row, lane):
    before = lax.rem(piece + PIECES - 1, PIECES)
    after = lax.rem(piece + 1, PIECES)
    here, left, right = get(piece, row), get(before, row), get(after, row)
    ahead, behind = [], []
    for k in (1, 2, 3):
        ahead.append(pltpu.roll(jnp.where(lane < k, right, here), LANES - k, 1))
        behind.append(pltpu.roll(jnp.where(lane >= LANES - k, left, here), k, 1))
    return here, ahead, behind


def shifted_x(get, piece, row):
    return [get(piece, row + k) for k in (1, 2, 3)], [get(piece, row - k) for k in (1, 2, 3)]


def slope(ahead, behind):
    total = None
    for k in range(3):
        term = (-COURANT * SLOPE[k]) * (ahead[k] - behind[k])
        total = term if total is None else total + term
    return total


def weights(wind):
    plus, minus = [], []
    for k in range(3):
        carry = wind * (-COURANT * SLOPE[k])
        plus.append(DAMPING * SIXTH[k] + carry)
        minus.append(DAMPING * SIXTH[k] - carry)
    return plus, minus


def stencil(here, x_side, y_side, by_x, by_y):
    total = (1.0 - 40.0 * DAMPING) * here
    for (ahead, behind), (plus, minus) in ((x_side, by_x), (y_side, by_y)):
        for k in range(3):
            total = total + plus[k] * ahead[k]
            total = total + minus[k] * behind[k]
    return total


def reader(ref, field):
    def get(piece, row):
        return ref[field, piece, pl.ds(OFF + row, SUB), :]

    return get


def mass_stage(log_get, old, pressure, divergence, step, start, blocks, store):
    def run(piece, carry):
        lane = lanes()
        for block in range(blocks):
            row = start + SUB * block
            east = reader(old, 1)
            north = reader(old, 2)
            by_x = weights(east(piece, row))
            n_here, n_ahead, n_behind = shifted_y(north, piece, row, lane)
            by_y = weights(n_here)
            div = slope(*shifted_x(east, piece, row)) + slope(n_ahead, n_behind)
            g_here, g_ahead, g_behind = shifted_y(log_get, piece, row, lane)
            new = stencil(g_here, shifted_x(log_get, piece, row), (g_ahead, g_behind), by_x, by_y) + div
            thick = jnp.exp(new)
            at = pl.ds(OFF + row, SUB)
            divergence[step, piece, at, :] = div
            pressure[step, piece, at, :] = reader(old, 3)(piece, row) * thick
            store(piece, row, new, thick)
        return carry

    lax.fori_loop(0, PIECES, run, 0)


def wind_piece(old, pressure, step, piece, row, lane):
    east, north, temper, press = reader(old, 1), reader(old, 2), reader(old, 3), reader(pressure, step)
    e_here, e_ahead, e_behind = shifted_y(east, piece, row, lane)
    n_here, n_ahead, n_behind = shifted_y(north, piece, row, lane)
    by_x, by_y = weights(e_here), weights(n_here)
    new_east = stencil(e_here, shifted_x(east, piece, row), (e_ahead, e_behind), by_x, by_y)
    new_east = new_east + slope(*shifted_x(press, piece, row))
    new_north = stencil(n_here, shifted_x(north, piece, row), (n_ahead, n_behind), by_x, by_y)
    _, p_ahead, p_behind = shifted_y(press, piece, row, lane)
    new_north = new_north + slope(p_ahead, p_behind)
    t_here, t_ahead, t_behind = shifted_y(temper, piece, row, lane)
    new_temper = stencil(t_here, shifted_x(temper, piece, row), (t_ahead, t_behind), by_x, by_y)
    return new_east, new_north, new_temper


def passive_piece(old, divergence, step, piece, row, lane):
    by_x = weights(reader(old, 1)(piece, row))
    by_y = weights(reader(old, 2)(piece, row))
    out = []
    for field in (4, 5):
        get = reader(old, field)
        here, ahead, behind = shifted_y(get, piece, row, lane)
        out.append(stencil(here, shifted_x(get, piece, row), (ahead, behind), by_x, by_y))
    out[1] = out[1] + divergence[step, piece, pl.ds(OFF + row, SUB), :]
    return out


def stage(body, start, blocks, store):
    def run(piece, carry):
        lane = lanes()
        for block in range(blocks):
            row = start + SUB * block
            store(piece, row, body(piece, row, lane))
        return carry

    lax.fori_loop(0, PIECES, run, 0)


def advance_kernel(*refs):
    inputs = refs[:FIELDS]
    got_a, got_b = refs[FIELDS : FIELDS + 2]
    (state0, state1, state2, logs, pressure, divergence, out_a, out_b, z_send, z_recv, x_send, x_recv, far_send, far_recv, all_send, all_recv, own_sem, ready) = refs[FIELDS + 2 :]

    column, ring, core = place()
    high = lax.div(ring, 4)

    barrier = pltpu.get_barrier_semaphore()
    twin = device(column, ring, 1 - core)
    partners = [device(column + d, ring, core) for d in (2, -2, 1, -1)]
    partners += [device(column, ring + d, core) for d in (2, -2, 1, -1)] + [twin]
    for who in partners:
        pl.semaphore_signal(barrier, inc=1, device_id=who, device_id_type=MESH)
    pl.semaphore_wait(barrier, len(partners))

    half = pl.ds(pl.multiple_of(OFF + SUB * high, SUB), SUB)
    sends = []
    z_copies = []
    for field in range(FIELDS):
        pair = []
        for way, (level, hop) in enumerate(((high, 2), (1 - high, -2))):
            copy = pltpu.make_async_remote_copy(
                src_ref=inputs[field].at[level],
                dst_ref=state0.at[field, :, half, :],
                send_sem=z_send.at[field, way],
                recv_sem=z_recv.at[field, way],
                device_id=device(column, ring + hop, core),
                device_id_type=MESH,
            )
            pair.append(copy)
        z_copies.append(pair)

    for field in range(AHEAD):
        for copy in z_copies[field]:
            copy.start()

    x_copies = []
    for field in range(FIELDS):
        if field + AHEAD < FIELDS:
            for copy in z_copies[field]:
                copy.wait_send()
            for copy in z_copies[field + AHEAD]:
                copy.start()
        else:
            sends += z_copies[field]
        for copy in z_copies[field]:
            copy.wait_recv()
        if field == 0:
            pl.semaphore_signal(ready, inc=1, device_id=twin, device_id_type=MESH)
        group = []
        for way in (0, 1):
            first, count = REACH[field][way]
            shift = -16 if way == 0 else 16
            copy = pltpu.make_async_remote_copy(
                src_ref=state0.at[field, :, pl.ds(OFF + first, count), :],
                dst_ref=state0.at[field, :, pl.ds(OFF + first + shift, count), :],
                send_sem=x_send.at[field, way],
                recv_sem=x_recv.at[field, way],
                device_id=device(column + (1 if way == 0 else -1), ring, core),
                device_id_type=MESH,
            )
            copy.start()
            group.append(copy)
        if field < 2:
            for way in (0, 1):
                first, shift = (14, -32) if way == 0 else (0, 32)
                copy = pltpu.make_async_remote_copy(
                    src_ref=state0.at[field, :, pl.ds(OFF + first, 2), :],
                    dst_ref=state0.at[field, :, pl.ds(OFF + first + shift, 2), :],
                    send_sem=far_send.at[field, way],
                    recv_sem=far_recv.at[field, way],
                    device_id=device(column + (2 if way == 0 else -2), ring, core),
                    device_id_type=MESH,
                )
                copy.start()
                group.append(copy)
        x_copies.append(group)
        sends += group

    for copy in x_copies[0]:
        copy.wait_recv()

    def take_log(piece, carry):
        for block in range(7):
            at = pl.ds(OFF - 18 + SUB * block, SUB)
            logs[0, piece, at, :] = jnp.log(state0[0, piece, at, :])
        return carry

    lax.fori_loop(0, PIECES, take_log, 0)

    for field in (1, 2, 3):
        for copy in x_copies[field]:
            copy.wait_recv()

    def keep(ref, fields):
        def store(piece, row, values):
            for field, value in zip(fields, values):
                ref[field, piece, pl.ds(OFF + row, SUB), :] = value

        return store

    def keep_log(ref):
        def store(piece, row, new, thick):
            ref[0, piece, pl.ds(OFF + row, SUB), :] = new

        return store

    def keep_thick(piece, row, new, thick):
        logs[0, piece, pl.ds(OFF + row, SUB), :] = thick

    states = (state0, state1, state2)
    mass_stage(reader(logs, 0), state0, pressure, divergence, 0, -16, 6, keep_log(state1))
    stage(functools.partial(wind_piece, state0, pressure, 0), -12, 5, keep(state1, (1, 2, 3)))
    mass_stage(reader(state1, 0), state1, pressure, divergence, 1, -12, 5, keep_log(state2))
    stage(functools.partial(wind_piece, state1, pressure, 1), -8, 4, keep(state2, (1, 2, 3)))
    mass_stage(reader(state2, 0), state2, pressure, divergence, 2, -4, 3, keep_thick)

    pl.semaphore_wait(ready, 1)
    level = owned_level(ring, core)
    lev = lax.rem(ring, 4) * 2 + core

    def give(piece, part, out, got):
        for tile_half in (0, 1):
            mine = jnp.logical_and(piece == lev, high == tile_half)
            slot = piece * 2 + tile_half

            @pl.when(mine)
            def _():
                pltpu.make_async_copy(out.at[piece, tile_half], got.at[level], own_sem.at[part]).start()

            @pl.when(jnp.logical_not(mine))
            def _():
                pltpu.make_async_remote_copy(
                    src_ref=out.at[piece, tile_half],
                    dst_ref=got.at[level],
                    send_sem=all_send.at[part, slot],
                    recv_sem=all_recv.at[part, level],
                    device_id=(column * 2 + tile_half, piece),
                    device_id_type=MESH,
                ).start()

    def last_winds(turn, carry):
        piece = lax.rem(lax.rem(ring, 4) * 2 + turn, PIECES)
        lane = lanes()
        for tile_half in (0, 1):
            row = SUB * tile_half
            out_a[piece, tile_half, 0, :, :] = logs[0, piece, pl.ds(OFF + row, SUB), :]
            for n, value in enumerate(wind_piece(state2, pressure, 2, piece, row, lane)):
                out_a[piece, tile_half, n + 1, :, :] = value
        give(piece, 0, out_a, got_a)
        return carry

    lax.fori_loop(0, PIECES, last_winds, 0)

    for field in (4, 5):
        for copy in x_copies[field]:
            copy.wait_recv()

    stage(functools.partial(passive_piece, state0, divergence, 0), -8, 4, keep(state1, (4, 5)))
    stage(functools.partial(passive_piece, state1, divergence, 1), -4, 3, keep(state2, (4, 5)))

    def last_passive(turn, carry):
        piece = lax.rem(lax.rem(ring, 4) * 2 + turn, PIECES)
        lane = lanes()
        for tile_half in (0, 1):
            for n, value in enumerate(passive_piece(state2, divergence, 2, piece, SUB * tile_half, lane)):
                out_b[piece, tile_half, n, :, :] = value
        give(piece, 1, out_b, got_b)
        return carry

    lax.fori_loop(0, PIECES, last_passive, 0)

    for copy in sends:
        copy.wait_send()

    def finish(part, out, got):
        def run(slot, carry):
            @pl.when(slot != lev * 2 + high)
            def _():
                pltpu.make_async_copy(out.at[0, 0], out.at[0, 0], all_send.at[part, slot]).wait()

            @pl.when(slot != level)
            def _():
                pltpu.make_async_copy(got.at[slot], got.at[slot], all_recv.at[part, slot]).wait()

            return carry

        lax.fori_loop(0, LEVELS, run, 0)
        pltpu.make_async_copy(out.at[0, 0], got.at[0], own_sem.at[part]).wait()

    finish(0, out_a, got_a)
    finish(1, out_b, got_b)


def advance(fields):
    state = pltpu.VMEM((FIELDS, PIECES, ROWS, LANES), jnp.float32)
    return pl.pallas_call(
        advance_kernel,
        out_shape=(
            jax.ShapeDtypeStruct((LEVELS, 4, SUB, LANES), jnp.float32),
            jax.ShapeDtypeStruct((LEVELS, 2, SUB, LANES), jnp.float32),
        ),
        in_specs=[pl.BlockSpec(memory_space=pl.ANY)] * FIELDS,
        out_specs=(pl.BlockSpec(memory_space=pl.ANY), pl.BlockSpec(memory_space=pl.ANY)),
        scratch_shapes=[
            state,
            state,
            state,
            pltpu.VMEM((1, PIECES, ROWS, LANES), jnp.float32),
            pltpu.VMEM((3, PIECES, ROWS, LANES), jnp.float32),
            pltpu.VMEM((3, PIECES, ROWS, LANES), jnp.float32),
            pltpu.VMEM((PIECES, 2, 4, SUB, LANES), jnp.float32),
            pltpu.VMEM((PIECES, 2, 2, SUB, LANES), jnp.float32),
            pltpu.SemaphoreType.DMA((FIELDS, 2)),
            pltpu.SemaphoreType.DMA((FIELDS, 2)),
            pltpu.SemaphoreType.DMA((FIELDS, 2)),
            pltpu.SemaphoreType.DMA((FIELDS, 2)),
            pltpu.SemaphoreType.DMA((2, 2)),
            pltpu.SemaphoreType.DMA((2, 2)),
            pltpu.SemaphoreType.DMA((2, LEVELS)),
            pltpu.SemaphoreType.DMA((2, LEVELS)),
            pltpu.SemaphoreType.DMA((2,)),
            pltpu.SemaphoreType.REGULAR,
        ],
        name="advance",
        compiler_params=pltpu.CompilerParams(
            collective_id=0, has_side_effects=True, vmem_limit_bytes=60 * 1024 * 1024
        ),
    )(*fields)


def remap_kernel(got_a, got_b, index_ref, slot_ref, *outs):
    thick = [got_a[k, 0] for k in range(LEVELS)]
    before = [jnp.zeros_like(thick[0])]
    for k in range(LEVELS):
        before.append(before[-1] + thick[k])
    picks, parts = [], []
    mass = [before[0]]
    for j in range(1, LEVELS):
        upper = index_ref[j - 1] == j
        x = slot_ref[j - 1].astype(jnp.float32) * (1.0 / SLOTS)
        square = 0.5 * x * x
        bend = square - x * x * x * (1.0 / 3.0)
        at = jnp.where(upper, thick[j], thick[j - 1])
        mass.append(jnp.where(upper, before[j], before[j - 1]) + x * at)
        picks.append(upper)
        parts.append((at, x - square - 3.0 * bend, square - 3.0 * bend, 6.0 * bend))
    mass.append(before[LEVELS])
    layer = []
    for j in range(LEVELS):
        layer.append(mass[j + 1] - mass[j])
        outs[0][j] = layer[j]
    for field in range(5):
        if field < 3:
            f = [got_a[k, field + 1] for k in range(LEVELS)]
        else:
            f = [got_b[k, field - 3] for k in range(LEVELS)]
        edge = [f[0], 0.5 * (f[0] + f[1])]
        for k in range(2, LEVELS - 1):
            edge.append((7.0 * (f[k - 1] + f[k]) - (f[k - 2] + f[k + 1])) * (1.0 / 12.0))
        edge += [0.5 * (f[-2] + f[-1]), f[-1]]
        running = jnp.zeros_like(f[0])
        sums = [running]
        for k in range(LEVELS):
            running = running + thick[k] * f[k]
            sums.append(running)
        last = sums[0]
        for j in range(1, LEVELS + 1):
            if j < LEVELS:
                upper = picks[j - 1]
                at, w_left, w_right, w_mid = parts[j - 1]
                left = jnp.where(upper, edge[j], edge[j - 1])
                right = jnp.where(upper, edge[j + 1], edge[j])
                mid = jnp.where(upper, f[j], f[j - 1])
                base = jnp.where(upper, sums[j], sums[j - 1])
                content = base + at * (w_left * left + w_right * right + w_mid * mid)
            else:
                content = sums[LEVELS]
            outs[field + 1][j - 1] = (content - last) / layer[j - 1]
            last = content


def remap(got_a, got_b, index, slot):
    vmem = pl.BlockSpec(memory_space=pltpu.VMEM)
    return pl.pallas_call(
        remap_kernel,
        out_shape=tuple(jax.ShapeDtypeStruct((LEVELS, SUB, LANES), jnp.float32) for _ in range(6)),
        in_specs=[vmem] * 4,
        out_specs=tuple([vmem] * 6),
        name="remap",
    )(got_a, got_b, index, slot)


def body(thickness, wind_east, wind_north, theta, tracer, wind_vertical, cross_index, cross_slot):
    fields = [
        f.reshape(2, SUB, PIECES, LANES).transpose(0, 2, 1, 3)
        for f in (thickness, wind_east, wind_north, theta, tracer, wind_vertical)
    ]
    got_a, got_b = advance(fields)
    return tuple(remap(got_a, got_b, cross_index, cross_slot))


def solution(mesh):
    split = P("lev", "tile", None)
    joined = P(None, "tile", "lev")
    return jax.shard_map(
        body,
        mesh=mesh,
        in_specs=(split,) * 6 + (joined,) * 2,
        out_specs=(joined,) * 6,
        check_vma=False,
    )
```

```python
import functools

import jax
import jax.numpy as jnp
from jax import lax
from jax.experimental import pallas as pl
from jax.experimental.pallas import tpu as pltpu
from jax.sharding import PartitionSpec as P

MESH = pl.DeviceIdType.MESH

COURANT = 0.1
DAMPING = 0.015
SLOPE = (45.0 / 60.0, -9.0 / 60.0, 1.0 / 60.0)
SIXTH = (15.0, -6.0, 1.0)
SLOTS = 8

LANES = 128
SUB = 8
PIECES = 8
LEVELS = 16
FIELDS = 6
PARTS = 3
COLUMNS = 16
OFF = 24
ROWS = 64
AHEAD = 2
UNROLL = 8

REACH = (((0, 16), (0, 16)), ((0, 16), (0, 16)), ((1, 15), (0, 15)), ((1, 15), (0, 15)), ((7, 9), (0, 9)), ((7, 9), (0, 9)))


def place():
    tile = lax.axis_index("tile")
    lev = lax.axis_index("lev")
    high = lax.rem(tile, 2)
    column = lax.div(tile, 2)
    ring = high * 4 + lax.div(lev, 2)
    core = lax.rem(lev, 2)
    return column, ring, core


def device(column, ring, core):
    column = lax.rem(column + 2 * COLUMNS, COLUMNS)
    ring = lax.rem(ring + 16, 8)
    return (column * 2 + lax.div(ring, 4), lax.rem(ring, 4) * 2 + core)


def owned_level(ring, core):
    first = jnp.logical_and(ring >= 2, ring < 6)
    early = 4 * (ring - 2) + 2 * core
    late = 4 * lax.rem(ring + 2, 8) + 2 * core + 1
    return jnp.where(first, early, late)


def lanes():
    return lax.broadcasted_iota(jnp.int32, (SUB, LANES), 1)


def shifted_y(get, piece, row, lane):
    before = lax.rem(piece + PIECES - 1, PIECES)
    after = lax.rem(piece + 1, PIECES)
    here, left, right = get(piece, row), get(before, row), get(after, row)
    ahead, behind = [], []
    for k in (1, 2, 3):
        ahead.append(pltpu.roll(jnp.where(lane < k, right, here), LANES - k, 1))
        behind.append(pltpu.roll(jnp.where(lane >= LANES - k, left, here), k, 1))
    return here, ahead, behind


def shifted_x(get, piece, row):
    return [get(piece, row + k) for k in (1, 2, 3)], [get(piece, row - k) for k in (1, 2, 3)]


def slope(ahead, behind):
    total = None
    for k in range(3):
        term = (-COURANT * SLOPE[k]) * (ahead[k] - behind[k])
        total = term if total is None else total + term
    return total


def weights(wind):
    plus, minus = [], []
    for k in range(3):
        carry = wind * (-COURANT * SLOPE[k])
        plus.append(DAMPING * SIXTH[k] + carry)
        minus.append(DAMPING * SIXTH[k] - carry)
    return plus, minus


def stencil(here, x_side, y_side, by_x, by_y):
    total = (1.0 - 40.0 * DAMPING) * here
    for (ahead, behind), (plus, minus) in ((x_side, by_x), (y_side, by_y)):
        for k in range(3):
            total = total + plus[k] * ahead[k]
            total = total + minus[k] * behind[k]
    return total


def reader(ref, field):
    def get(piece, row):
        return ref[field, piece, pl.ds(OFF + row, SUB), :]

    return get


def mass_piece(log_get, old, pressure, divergence, step, piece, row, lane, store, with_theta):
    east = reader(old, 1)
    north = reader(old, 2)
    by_x = weights(east(piece, row))
    n_here, n_ahead, n_behind = shifted_y(north, piece, row, lane)
    by_y = weights(n_here)
    div = slope(*shifted_x(east, piece, row)) + slope(n_ahead, n_behind)
    g_here, g_ahead, g_behind = shifted_y(log_get, piece, row, lane)
    new = stencil(g_here, shifted_x(log_get, piece, row), (g_ahead, g_behind), by_x, by_y) + div
    thick = jnp.exp(new)
    at = pl.ds(OFF + row, SUB)
    divergence[step, piece, at, :] = div
    pressure[step, piece, at, :] = reader(old, 3)(piece, row) * thick if with_theta else thick
    store(piece, row, new, thick)


def mass_stage(log_get, old, pressure, divergence, step, start, blocks, store, with_theta=True):
    def run(piece, carry):
        lane = lanes()
        for block in range(blocks):
            mass_piece(log_get, old, pressure, divergence, step, piece, start + SUB * block, lane, store, with_theta)
        return carry

    lax.fori_loop(0, PIECES, run, 0, unroll=UNROLL)


def wind_piece(old, pressure, step, piece, row, lane, with_theta=True):
    east, north, temper, press = reader(old, 1), reader(old, 2), reader(old, 3), reader(pressure, step)
    e_here, e_ahead, e_behind = shifted_y(east, piece, row, lane)
    n_here, n_ahead, n_behind = shifted_y(north, piece, row, lane)
    by_x, by_y = weights(e_here), weights(n_here)
    new_east = stencil(e_here, shifted_x(east, piece, row), (e_ahead, e_behind), by_x, by_y)
    new_east = new_east + slope(*shifted_x(press, piece, row))
    new_north = stencil(n_here, shifted_x(north, piece, row), (n_ahead, n_behind), by_x, by_y)
    _, p_ahead, p_behind = shifted_y(press, piece, row, lane)
    new_north = new_north + slope(p_ahead, p_behind)
    if not with_theta:
        return new_east, new_north
    t_here, t_ahead, t_behind = shifted_y(temper, piece, row, lane)
    new_temper = stencil(t_here, shifted_x(temper, piece, row), (t_ahead, t_behind), by_x, by_y)
    return new_east, new_north, new_temper


def theta_piece(old, piece, row, lane):
    by_x = weights(reader(old, 1)(piece, row))
    by_y = weights(reader(old, 2)(piece, row))
    get = reader(old, 3)
    here, ahead, behind = shifted_y(get, piece, row, lane)
    return stencil(here, shifted_x(get, piece, row), (ahead, behind), by_x, by_y)


def passive_piece(old, divergence, step, piece, row, lane):
    by_x = weights(reader(old, 1)(piece, row))
    by_y = weights(reader(old, 2)(piece, row))
    out = []
    for field in (4, 5):
        get = reader(old, field)
        here, ahead, behind = shifted_y(get, piece, row, lane)
        out.append(stencil(here, shifted_x(get, piece, row), (ahead, behind), by_x, by_y))
    out[1] = out[1] + divergence[step, piece, pl.ds(OFF + row, SUB), :]
    return out


def stage(body, start, blocks, store):
    def run(piece, carry):
        lane = lanes()
        for block in range(blocks):
            row = start + SUB * block
            store(piece, row, body(piece, row, lane))
        return carry

    lax.fori_loop(0, PIECES, run, 0, unroll=UNROLL)


def advance_kernel(*refs):
    inputs = refs[:FIELDS]
    got = refs[FIELDS]
    (state0, state1, state2, logs, pressure, divergence, outgoing, z_send, z_recv, x_send, x_recv, far_send, far_recv, all_send, all_recv, own_sem, ready) = refs[FIELDS + 1 :]

    column, ring, core = place()
    high = lax.div(ring, 4)

    barrier = pltpu.get_barrier_semaphore()
    twin = device(column, ring, 1 - core)
    partners = [device(column + d, ring, core) for d in (2, -2, 1, -1)]
    partners += [device(column, ring + d, core) for d in (2, -2, 1, -1)] + [twin]
    for who in partners:
        pl.semaphore_signal(barrier, inc=1, device_id=who, device_id_type=MESH)
    pl.semaphore_wait(barrier, len(partners))

    half = pl.ds(pl.multiple_of(OFF + SUB * high, SUB), SUB)
    sends = []
    z_copies = []
    for field in range(FIELDS):
        pair = []
        for way, (level, hop) in enumerate(((high, 2), (1 - high, -2))):
            copy = pltpu.make_async_remote_copy(
                src_ref=inputs[field].at[level],
                dst_ref=state0.at[field, :, half, :],
                send_sem=z_send.at[field, way],
                recv_sem=z_recv.at[field, way],
                device_id=device(column, ring + hop, core),
                device_id_type=MESH,
            )
            pair.append(copy)
        z_copies.append(pair)

    for field in range(AHEAD):
        for copy in z_copies[field]:
            copy.start()

    x_copies = []

    def pass_on(field):
        if field + AHEAD < FIELDS:
            for copy in z_copies[field]:
                copy.wait_send()
            for copy in z_copies[field + AHEAD]:
                copy.start()
        else:
            sends.extend(z_copies[field])
        for copy in z_copies[field]:
            copy.wait_recv()
        if field == 0:
            pl.semaphore_signal(ready, inc=1, device_id=twin, device_id_type=MESH)
        group = []
        for way in (0, 1):
            first, count = REACH[field][way]
            shift = -16 if way == 0 else 16
            copy = pltpu.make_async_remote_copy(
                src_ref=state0.at[field, :, pl.ds(OFF + first, count), :],
                dst_ref=state0.at[field, :, pl.ds(OFF + first + shift, count), :],
                send_sem=x_send.at[field, way],
                recv_sem=x_recv.at[field, way],
                device_id=device(column + (1 if way == 0 else -1), ring, core),
                device_id_type=MESH,
            )
            copy.start()
            group.append(copy)
        if field < 2:
            for way in (0, 1):
                first, shift = (14, -32) if way == 0 else (0, 32)
                copy = pltpu.make_async_remote_copy(
                    src_ref=state0.at[field, :, pl.ds(OFF + first, 2), :],
                    dst_ref=state0.at[field, :, pl.ds(OFF + first + shift, 2), :],
                    send_sem=far_send.at[field, way],
                    recv_sem=far_recv.at[field, way],
                    device_id=device(column + (2 if way == 0 else -2), ring, core),
                    device_id_type=MESH,
                )
                copy.start()
                group.append(copy)
        x_copies.append(group)
        sends.extend(group)

    for field in range(4):
        pass_on(field)

    for copy in x_copies[0]:
        copy.wait_recv()

    def take_log(piece, carry):
        for block in range(7):
            at = pl.ds(OFF - 18 + SUB * block, SUB)
            logs[0, piece, at, :] = jnp.log(state0[0, piece, at, :])
        return carry

    lax.fori_loop(0, PIECES, take_log, 0, unroll=UNROLL)

    for field in (1, 2):
        for copy in x_copies[field]:
            copy.wait_recv()

    def keep(ref, fields):
        def store(piece, row, values):
            for field, value in zip(fields, values):
                ref[field, piece, pl.ds(OFF + row, SUB), :] = value

        return store

    def keep_log(ref):
        def store(piece, row, new, thick):
            ref[0, piece, pl.ds(OFF + row, SUB), :] = new

        return store

    def keep_thick(piece, row, new, thick):
        logs[0, piece, pl.ds(OFF + row, SUB), :] = thick

    mass_stage(reader(logs, 0), state0, pressure, divergence, 0, -16, 6, keep_log(state1), with_theta=False)

    pass_on(4)
    pass_on(5)

    for copy in x_copies[3]:
        copy.wait_recv()

    def times_theta(piece, row, lane):
        return (pressure[0, piece, pl.ds(OFF + row, SUB), :] * reader(state0, 3)(piece, row),)

    stage(times_theta, -16, 6, keep(pressure, (0,)))
    stage(functools.partial(wind_piece, state0, pressure, 0), -12, 5, keep(state1, (1, 2, 3)))
    mass_stage(reader(state1, 0), state1, pressure, divergence, 1, -12, 5, keep_log(state2))
    stage(functools.partial(wind_piece, state1, pressure, 1), -8, 4, keep(state2, (1, 2, 3)))
    pl.semaphore_wait(ready, 1)
    level = owned_level(ring, core)
    lev = lax.rem(ring, 4) * 2 + core

    def give(piece, part):
        out = outgoing.at[part]
        for tile_half in (0, 1):
            mine = jnp.logical_and(piece == lev, high == tile_half)
            slot = piece * 2 + tile_half

            @pl.when(mine)
            def _():
                pltpu.make_async_copy(out.at[piece, tile_half], got.at[part, level], own_sem.at[part]).start()

            @pl.when(jnp.logical_not(mine))
            def _():
                pltpu.make_async_remote_copy(
                    src_ref=out.at[piece, tile_half],
                    dst_ref=got.at[part, level],
                    send_sem=all_send.at[part, slot],
                    recv_sem=all_recv.at[part, level],
                    device_id=(column * 2 + tile_half, piece),
                    device_id_type=MESH,
                ).start()

    def turned(turn):
        return lax.rem(lax.rem(ring, 4) * 2 + turn, PIECES)

    def last_mass(turn, carry):
        piece = turned(turn)
        lane = lanes()
        for block in range(3):
            mass_piece(reader(state2, 0), state2, pressure, divergence, 2, piece, -4 + SUB * block, lane, keep_thick, True)
        for tile_half in (0, 1):
            row = SUB * tile_half
            outgoing[0, piece, tile_half, 0, :, :] = logs[0, piece, pl.ds(OFF + row, SUB), :]
            outgoing[0, piece, tile_half, 1, :, :] = theta_piece(state2, piece, row, lane)
        give(piece, 0)
        return carry

    lax.fori_loop(0, PIECES, last_mass, 0, unroll=UNROLL)

    def last_winds(turn, carry):
        piece = turned(turn)
        lane = lanes()
        for tile_half in (0, 1):
            for n, value in enumerate(wind_piece(state2, pressure, 2, piece, SUB * tile_half, lane, False)):
                outgoing[1, piece, tile_half, n, :, :] = value
        give(piece, 1)
        return carry

    lax.fori_loop(0, PIECES, last_winds, 0, unroll=UNROLL)

    for field in (4, 5):
        for copy in x_copies[field]:
            copy.wait_recv()

    stage(functools.partial(passive_piece, state0, divergence, 0), -8, 4, keep(state1, (4, 5)))
    stage(functools.partial(passive_piece, state1, divergence, 1), -4, 3, keep(state2, (4, 5)))

    def last_passive(turn, carry):
        piece = turned(turn)
        lane = lanes()
        for tile_half in (0, 1):
            for n, value in enumerate(passive_piece(state2, divergence, 2, piece, SUB * tile_half, lane)):
                outgoing[2, piece, tile_half, n, :, :] = value
        give(piece, 2)
        return carry

    lax.fori_loop(0, PIECES, last_passive, 0, unroll=UNROLL)

    for copy in sends:
        copy.wait_send()

    def finish(part):
        out = outgoing.at[part]

        def run(slot, carry):
            @pl.when(slot != lev * 2 + high)
            def _():
                pltpu.make_async_copy(out.at[0, 0], out.at[0, 0], all_send.at[part, slot]).wait()

            @pl.when(slot != level)
            def _():
                pltpu.make_async_copy(got.at[part, slot], got.at[part, slot], all_recv.at[part, slot]).wait()

            return carry

        lax.fori_loop(0, LEVELS, run, 0)
        pltpu.make_async_copy(out.at[0, 0], got.at[part, 0], own_sem.at[part]).wait()

    for part in range(PARTS):
        finish(part)


def advance(fields):
    state = pltpu.VMEM((FIELDS, PIECES, ROWS, LANES), jnp.float32)
    return pl.pallas_call(
        advance_kernel,
        out_shape=jax.ShapeDtypeStruct((PARTS, LEVELS, 2, SUB, LANES), jnp.float32),
        in_specs=[pl.BlockSpec(memory_space=pl.ANY)] * FIELDS,
        out_specs=pl.BlockSpec(memory_space=pl.ANY),
        scratch_shapes=[
            state,
            state,
            state,
            pltpu.VMEM((1, PIECES, ROWS, LANES), jnp.float32),
            pltpu.VMEM((3, PIECES, ROWS, LANES), jnp.float32),
            pltpu.VMEM((3, PIECES, ROWS, LANES), jnp.float32),
            pltpu.VMEM((PARTS, PIECES, 2, 2, SUB, LANES), jnp.float32),
            pltpu.SemaphoreType.DMA((FIELDS, 2)),
            pltpu.SemaphoreType.DMA((FIELDS, 2)),
            pltpu.SemaphoreType.DMA((FIELDS, 2)),
            pltpu.SemaphoreType.DMA((FIELDS, 2)),
            pltpu.SemaphoreType.DMA((2, 2)),
            pltpu.SemaphoreType.DMA((2, 2)),
            pltpu.SemaphoreType.DMA((PARTS, LEVELS)),
            pltpu.SemaphoreType.DMA((PARTS, LEVELS)),
            pltpu.SemaphoreType.DMA((PARTS,)),
            pltpu.SemaphoreType.REGULAR,
        ],
        name="advance",
        compiler_params=pltpu.CompilerParams(
            collective_id=0, has_side_effects=True, vmem_limit_bytes=60 * 1024 * 1024
        ),
    )(*fields)


def remap_kernel(got, index_ref, slot_ref, *outs):
    thick = [got[0, k, 0] for k in range(LEVELS)]
    before = [jnp.zeros_like(thick[0])]
    for k in range(LEVELS):
        before.append(before[-1] + thick[k])
    picks, parts = [], []
    mass = [before[0]]
    for j in range(1, LEVELS):
        upper = index_ref[j - 1] == j
        x = slot_ref[j - 1].astype(jnp.float32) * (1.0 / SLOTS)
        square = 0.5 * x * x
        bend = square - x * x * x * (1.0 / 3.0)
        at = jnp.where(upper, thick[j], thick[j - 1])
        mass.append(jnp.where(upper, before[j], before[j - 1]) + x * at)
        picks.append(upper)
        parts.append((at, x - square - 3.0 * bend, square - 3.0 * bend, 6.0 * bend))
    mass.append(before[LEVELS])
    layer = []
    for j in range(LEVELS):
        layer.append(mass[j + 1] - mass[j])
        outs[0][j] = layer[j]
    for field in range(5):
        part, n = ((1, 0), (1, 1), (0, 1), (2, 0), (2, 1))[field]
        f = [got[part, k, n] for k in range(LEVELS)]
        edge = [f[0], 0.5 * (f[0] + f[1])]
        for k in range(2, LEVELS - 1):
            edge.append((7.0 * (f[k - 1] + f[k]) - (f[k - 2] + f[k + 1])) * (1.0 / 12.0))
        edge += [0.5 * (f[-2] + f[-1]), f[-1]]
        running = jnp.zeros_like(f[0])
        sums = [running]
        for k in range(LEVELS):
            running = running + thick[k] * f[k]
            sums.append(running)
        last = sums[0]
        for j in range(1, LEVELS + 1):
            if j < LEVELS:
                upper = picks[j - 1]
                at, w_left, w_right, w_mid = parts[j - 1]
                left = jnp.where(upper, edge[j], edge[j - 1])
                right = jnp.where(upper, edge[j + 1], edge[j])
                mid = jnp.where(upper, f[j], f[j - 1])
                base = jnp.where(upper, sums[j], sums[j - 1])
                content = base + at * (w_left * left + w_right * right + w_mid * mid)
            else:
                content = sums[LEVELS]
            outs[field + 1][j - 1] = (content - last) / layer[j - 1]
            last = content


def remap(got, index, slot):
    vmem = pl.BlockSpec(memory_space=pltpu.VMEM)
    return pl.pallas_call(
        remap_kernel,
        out_shape=tuple(jax.ShapeDtypeStruct((LEVELS, SUB, LANES), jnp.float32) for _ in range(6)),
        in_specs=[vmem] * 3,
        out_specs=tuple([vmem] * 6),
        name="remap",
    )(got, index, slot)


def body(thickness, wind_east, wind_north, theta, tracer, wind_vertical, cross_index, cross_slot):
    fields = [
        f.reshape(2, SUB, PIECES, LANES).transpose(0, 2, 1, 3)
        for f in (thickness, wind_east, wind_north, theta, tracer, wind_vertical)
    ]
    return tuple(remap(advance(fields), cross_index, cross_slot))


def solution(mesh):
    split = P("lev", "tile", None)
    joined = P(None, "tile", "lev")
    return jax.shard_map(
        body,
        mesh=mesh,
        in_specs=(split,) * 6 + (joined,) * 2,
        out_specs=(joined,) * 6,
        check_vma=False,
    )
```

```python
import functools

import jax
import jax.numpy as jnp
from jax import lax
from jax.experimental import pallas as pl
from jax.experimental.pallas import tpu as pltpu
from jax.sharding import PartitionSpec as P

MESH = pl.DeviceIdType.MESH

COURANT = 0.1
DAMPING = 0.015
SLOPE = (45.0 / 60.0, -9.0 / 60.0, 1.0 / 60.0)
SIXTH = (15.0, -6.0, 1.0)
SLOTS = 8

LANES = 128
SUB = 8
PIECES = 8
LEVELS = 16
FIELDS = 6
PARTS = 3
COLUMNS = 16
OFF = 24
ROWS = 64
AHEAD = 2
CUTS = 1
UNROLL = 8

REACH = (((0, 16), (0, 16)), ((0, 16), (0, 16)), ((1, 15), (0, 15)), ((1, 15), (0, 15)), ((7, 9), (0, 9)), ((7, 9), (0, 9)))


def place():
    tile = lax.axis_index("tile")
    lev = lax.axis_index("lev")
    high = lax.rem(tile, 2)
    column = lax.div(tile, 2)
    ring = high * 4 + lax.div(lev, 2)
    core = lax.rem(lev, 2)
    return column, ring, core


def device(column, ring, core):
    column = lax.rem(column + 2 * COLUMNS, COLUMNS)
    ring = lax.rem(ring + 16, 8)
    return (column * 2 + lax.div(ring, 4), lax.rem(ring, 4) * 2 + core)


def owned_level(ring, core):
    first = jnp.logical_and(ring >= 2, ring < 6)
    early = 4 * (ring - 2) + 2 * core
    late = 4 * lax.rem(ring + 2, 8) + 2 * core + 1
    return jnp.where(first, early, late)


def lanes():
    return lax.broadcasted_iota(jnp.int32, (SUB, LANES), 1)


def shifted_y(get, piece, row, lane):
    before = lax.rem(piece + PIECES - 1, PIECES)
    after = lax.rem(piece + 1, PIECES)
    here, left, right = get(piece, row), get(before, row), get(after, row)
    ahead, behind = [], []
    for k in (1, 2, 3):
        ahead.append(pltpu.roll(jnp.where(lane < k, right, here), LANES - k, 1))
        behind.append(pltpu.roll(jnp.where(lane >= LANES - k, left, here), k, 1))
    return here, ahead, behind


def shifted_x(get, piece, row):
    return [get(piece, row + k) for k in (1, 2, 3)], [get(piece, row - k) for k in (1, 2, 3)]


def slope(ahead, behind):
    total = None
    for k in range(3):
        term = (-COURANT * SLOPE[k]) * (ahead[k] - behind[k])
        total = term if total is None else total + term
    return total


def weights(wind):
    plus, minus = [], []
    for k in range(3):
        carry = wind * (-COURANT * SLOPE[k])
        plus.append(DAMPING * SIXTH[k] + carry)
        minus.append(DAMPING * SIXTH[k] - carry)
    return plus, minus


def stencil(here, x_side, y_side, by_x, by_y):
    total = (1.0 - 40.0 * DAMPING) * here
    for (ahead, behind), (plus, minus) in ((x_side, by_x), (y_side, by_y)):
        for k in range(3):
            total = total + plus[k] * ahead[k]
            total = total + minus[k] * behind[k]
    return total


def reader(ref, field):
    def get(piece, row):
        return ref[field, piece, pl.ds(OFF + row, SUB), :]

    return get


def mass_piece(log_get, old, pressure, divergence, step, piece, row, lane, store, with_theta):
    east = reader(old, 1)
    north = reader(old, 2)
    by_x = weights(east(piece, row))
    n_here, n_ahead, n_behind = shifted_y(north, piece, row, lane)
    by_y = weights(n_here)
    div = slope(*shifted_x(east, piece, row)) + slope(n_ahead, n_behind)
    g_here, g_ahead, g_behind = shifted_y(log_get, piece, row, lane)
    new = stencil(g_here, shifted_x(log_get, piece, row), (g_ahead, g_behind), by_x, by_y) + div
    thick = jnp.exp(new)
    at = pl.ds(OFF + row, SUB)
    divergence[step, piece, at, :] = div
    pressure[step, piece, at, :] = reader(old, 3)(piece, row) * thick if with_theta else thick
    store(piece, row, new, thick)


def mass_stage(log_get, old, pressure, divergence, step, start, blocks, store, with_theta=True):
    def run(piece, carry):
        lane = lanes()
        for block in range(blocks):
            mass_piece(log_get, old, pressure, divergence, step, piece, start + SUB * block, lane, store, with_theta)
        return carry

    lax.fori_loop(0, PIECES, run, 0, unroll=UNROLL)


def wind_piece(old, pressure, step, piece, row, lane, with_theta=True):
    east, north, temper, press = reader(old, 1), reader(old, 2), reader(old, 3), reader(pressure, step)
    e_here, e_ahead, e_behind = shifted_y(east, piece, row, lane)
    n_here, n_ahead, n_behind = shifted_y(north, piece, row, lane)
    by_x, by_y = weights(e_here), weights(n_here)
    new_east = stencil(e_here, shifted_x(east, piece, row), (e_ahead, e_behind), by_x, by_y)
    new_east = new_east + slope(*shifted_x(press, piece, row))
    new_north = stencil(n_here, shifted_x(north, piece, row), (n_ahead, n_behind), by_x, by_y)
    _, p_ahead, p_behind = shifted_y(press, piece, row, lane)
    new_north = new_north + slope(p_ahead, p_behind)
    if not with_theta:
        return new_east, new_north
    t_here, t_ahead, t_behind = shifted_y(temper, piece, row, lane)
    new_temper = stencil(t_here, shifted_x(temper, piece, row), (t_ahead, t_behind), by_x, by_y)
    return new_east, new_north, new_temper


def theta_piece(old, piece, row, lane):
    by_x = weights(reader(old, 1)(piece, row))
    by_y = weights(reader(old, 2)(piece, row))
    get = reader(old, 3)
    here, ahead, behind = shifted_y(get, piece, row, lane)
    return stencil(here, shifted_x(get, piece, row), (ahead, behind), by_x, by_y)


def passive_piece(old, divergence, step, piece, row, lane):
    by_x = weights(reader(old, 1)(piece, row))
    by_y = weights(reader(old, 2)(piece, row))
    out = []
    for field in (4, 5):
        get = reader(old, field)
        here, ahead, behind = shifted_y(get, piece, row, lane)
        out.append(stencil(here, shifted_x(get, piece, row), (ahead, behind), by_x, by_y))
    out[1] = out[1] + divergence[step, piece, pl.ds(OFF + row, SUB), :]
    return out


def stage(body, start, blocks, store):
    def run(piece, carry):
        lane = lanes()
        for block in range(blocks):
            row = start + SUB * block
            store(piece, row, body(piece, row, lane))
        return carry

    lax.fori_loop(0, PIECES, run, 0, unroll=UNROLL)


def advance_kernel(*refs):
    inputs = refs[:FIELDS]
    got = refs[FIELDS]
    (state0, state1, state2, logs, pressure, divergence, outgoing, z_send, z_recv, x_send, x_recv, all_send, all_recv, own_sem, ready) = refs[FIELDS + 1 :]

    column, ring, core = place()
    high = lax.div(ring, 4)

    barrier = pltpu.get_barrier_semaphore()
    twin = device(column, ring, 1 - core)
    partners = [device(column + d, ring, core) for d in (2, -2, 1, -1)]
    partners += [device(column, ring + d, core) for d in (2, -2, 1, -1)] + [twin]
    for who in partners:
        pl.semaphore_signal(barrier, inc=1, device_id=who, device_id_type=MESH)
    pl.semaphore_wait(barrier, len(partners))

    half = pl.ds(pl.multiple_of(OFF + SUB * high, SUB), SUB)
    sends = []
    cut = PIECES // CUTS
    z_copies = []
    for n in range(FIELDS * CUTS):
        field, span = n // CUTS, pl.ds(n % CUTS * cut, cut)
        pair = []
        for way, (level, hop) in enumerate(((high, 2), (1 - high, -2))):
            pair.append(
                pltpu.make_async_remote_copy(
                    src_ref=inputs[field].at[level, span],
                    dst_ref=state0.at[field, span, half, :],
                    send_sem=z_send.at[n, way],
                    recv_sem=z_recv.at[n, way],
                    device_id=device(column, ring + hop, core),
                    device_id_type=MESH,
                )
            )
        z_copies.append(pair)

    for pair in z_copies[:AHEAD]:
        for copy in pair:
            copy.start()

    x_copies = [[] for _ in range(FIELDS)]

    def pass_on(n):
        field, span = n // CUTS, pl.ds(n % CUTS * cut, cut)
        if n + AHEAD < FIELDS * CUTS:
            for copy in z_copies[n]:
                copy.wait_send()
            for copy in z_copies[n + AHEAD]:
                copy.start()
        else:
            sends.extend(z_copies[n])
        for copy in z_copies[n]:
            copy.wait_recv()
        if n == 0:
            pl.semaphore_signal(ready, inc=1, device_id=twin, device_id_type=MESH)
        routes = [(way, hop, REACH[field][way], shift) for way, hop, shift in ((0, 1, -16), (1, -1, 16))]
        if field < 2:
            routes += [(2, 2, (14, 2), -32), (3, -2, (0, 2), 32)]
        for way, hop, (first, count), shift in routes:
            copy = pltpu.make_async_remote_copy(
                src_ref=state0.at[field, span, pl.ds(OFF + first, count), :],
                dst_ref=state0.at[field, span, pl.ds(OFF + first + shift, count), :],
                send_sem=x_send.at[n, way],
                recv_sem=x_recv.at[n, way],
                device_id=device(column + hop, ring, core),
                device_id_type=MESH,
            )
            copy.start()
            x_copies[field].append(copy)
            sends.append(copy)

    for n in range(4 * CUTS):
        pass_on(n)

    for copy in x_copies[0]:
        copy.wait_recv()

    def take_log(piece, carry):
        for block in range(7):
            at = pl.ds(OFF - 18 + SUB * block, SUB)
            logs[0, piece, at, :] = jnp.log(state0[0, piece, at, :])
        return carry

    lax.fori_loop(0, PIECES, take_log, 0, unroll=UNROLL)

    for field in (1, 2):
        for copy in x_copies[field]:
            copy.wait_recv()

    def keep(ref, fields):
        def store(piece, row, values):
            for field, value in zip(fields, values):
                ref[field, piece, pl.ds(OFF + row, SUB), :] = value

        return store

    def keep_log(ref):
        def store(piece, row, new, thick):
            ref[0, piece, pl.ds(OFF + row, SUB), :] = new

        return store

    def keep_thick(piece, row, new, thick):
        logs[0, piece, pl.ds(OFF + row, SUB), :] = thick

    mass_stage(reader(logs, 0), state0, pressure, divergence, 0, -16, 6, keep_log(state1), with_theta=False)

    for n in range(4 * CUTS, FIELDS * CUTS):
        pass_on(n)

    for copy in x_copies[3]:
        copy.wait_recv()

    def times_theta(piece, row, lane):
        return (pressure[0, piece, pl.ds(OFF + row, SUB), :] * reader(state0, 3)(piece, row),)

    stage(times_theta, -16, 6, keep(pressure, (0,)))
    stage(functools.partial(wind_piece, state0, pressure, 0), -12, 5, keep(state1, (1, 2, 3)))
    mass_stage(reader(state1, 0), state1, pressure, divergence, 1, -12, 5, keep_log(state2))
    stage(functools.partial(wind_piece, state1, pressure, 1), -8, 4, keep(state2, (1, 2, 3)))
    pl.semaphore_wait(ready, 1)
    level = owned_level(ring, core)
    lev = lax.rem(ring, 4) * 2 + core

    def give(piece, part, halves):
        out = outgoing.at[part]
        for tile_half in halves:
            mine = jnp.logical_and(piece == lev, high == tile_half)
            slot = piece * 2 + tile_half

            @pl.when(mine)
            def _():
                pltpu.make_async_copy(out.at[piece, tile_half], got.at[part, level], own_sem.at[part]).start()

            @pl.when(jnp.logical_not(mine))
            def _():
                pltpu.make_async_remote_copy(
                    src_ref=out.at[piece, tile_half],
                    dst_ref=got.at[part, level],
                    send_sem=all_send.at[part, slot],
                    recv_sem=all_recv.at[part, level],
                    device_id=(column * 2 + tile_half, piece),
                    device_id_type=MESH,
                ).start()

    def give_rest(part):
        def run(turn, carry):
            give(turned(turn), part, (1,))
            return carry

        lax.fori_loop(0, PIECES, run, 0)

    def turned(turn):
        return turn

    def last_mass(turn, carry):
        piece = turned(turn)
        lane = lanes()
        for block in range(3):
            mass_piece(reader(state2, 0), state2, pressure, divergence, 2, piece, -4 + SUB * block, lane, keep_thick, True)
        for tile_half in (0, 1):
            row = SUB * tile_half
            outgoing[0, piece, tile_half, 0, :, :] = logs[0, piece, pl.ds(OFF + row, SUB), :]
            outgoing[0, piece, tile_half, 1, :, :] = theta_piece(state2, piece, row, lane)
        give(piece, 0, (0,))
        return carry

    lax.fori_loop(0, PIECES, last_mass, 0, unroll=UNROLL)

    def last_winds(turn, carry):
        piece = turned(turn)
        lane = lanes()
        for tile_half in (0, 1):
            for n, value in enumerate(wind_piece(state2, pressure, 2, piece, SUB * tile_half, lane, False)):
                outgoing[1, piece, tile_half, n, :, :] = value
        give(piece, 1, (0,))
        return carry

    lax.fori_loop(0, PIECES, last_winds, 0, unroll=UNROLL)

    for field in (4, 5):
        for copy in x_copies[field]:
            copy.wait_recv()

    stage(functools.partial(passive_piece, state0, divergence, 0), -8, 4, keep(state1, (4, 5)))
    stage(functools.partial(passive_piece, state1, divergence, 1), -4, 3, keep(state2, (4, 5)))

    def last_passive(turn, carry):
        piece = turned(turn)
        lane = lanes()
        for tile_half in (0, 1):
            for n, value in enumerate(passive_piece(state2, divergence, 2, piece, SUB * tile_half, lane)):
                outgoing[2, piece, tile_half, n, :, :] = value
        give(piece, 2, (0,))
        return carry

    lax.fori_loop(0, PIECES, last_passive, 0, unroll=UNROLL)
    for part in range(PARTS):
        give_rest(part)

    for copy in sends:
        copy.wait_send()

    def sent(n, carry):
        part, slot = lax.div(n, LEVELS), lax.rem(n, LEVELS)

        @pl.when(slot != lev * 2 + high)
        def _():
            pltpu.make_async_copy(outgoing.at[0, 0, 0], outgoing.at[0, 0, 0], all_send.at[part, slot]).wait()

        return carry

    def arrived(n, carry):
        part, slot = lax.div(n, LEVELS), lax.rem(n, LEVELS)

        @pl.when(slot != level)
        def _():
            pltpu.make_async_copy(got.at[part, slot], got.at[part, slot], all_recv.at[part, slot]).wait()

        return carry

    lax.fori_loop(0, 2 * LEVELS, sent, 0)
    for part in range(PARTS):
        pltpu.make_async_copy(outgoing.at[part, 0, 0], got.at[part, 0], own_sem.at[part]).wait()
    lax.fori_loop(0, 2 * LEVELS, arrived, 0)
    lax.fori_loop(2 * LEVELS, 3 * LEVELS, sent, 0)
    lax.fori_loop(2 * LEVELS, 3 * LEVELS, arrived, 0)


def advance(fields):
    state = pltpu.VMEM((FIELDS, PIECES, ROWS, LANES), jnp.float32)
    return pl.pallas_call(
        advance_kernel,
        out_shape=jax.ShapeDtypeStruct((PARTS, LEVELS, 2, SUB, LANES), jnp.float32),
        in_specs=[pl.BlockSpec(memory_space=pl.ANY)] * FIELDS,
        out_specs=pl.BlockSpec(memory_space=pl.ANY),
        scratch_shapes=[
            state,
            state,
            state,
            pltpu.VMEM((1, PIECES, ROWS, LANES), jnp.float32),
            pltpu.VMEM((3, PIECES, ROWS, LANES), jnp.float32),
            pltpu.VMEM((3, PIECES, ROWS, LANES), jnp.float32),
            pltpu.VMEM((PARTS, PIECES, 2, 2, SUB, LANES), jnp.float32),
            pltpu.SemaphoreType.DMA((FIELDS * CUTS, 2)),
            pltpu.SemaphoreType.DMA((FIELDS * CUTS, 2)),
            pltpu.SemaphoreType.DMA((FIELDS * CUTS, 4)),
            pltpu.SemaphoreType.DMA((FIELDS * CUTS, 4)),
            pltpu.SemaphoreType.DMA((PARTS, LEVELS)),
            pltpu.SemaphoreType.DMA((PARTS, LEVELS)),
            pltpu.SemaphoreType.DMA((PARTS,)),
            pltpu.SemaphoreType.REGULAR,
        ],
        name="advance",
        compiler_params=pltpu.CompilerParams(
            collective_id=0, has_side_effects=True, vmem_limit_bytes=60 * 1024 * 1024
        ),
    )(*fields)


def remap_kernel(got, index_ref, slot_ref, *outs):
    thick = [got[0, k, 0] for k in range(LEVELS)]
    before = [jnp.zeros_like(thick[0])]
    for k in range(LEVELS):
        before.append(before[-1] + thick[k])
    picks, parts = [], []
    mass = [before[0]]
    for j in range(1, LEVELS):
        upper = index_ref[j - 1] == j
        x = slot_ref[j - 1].astype(jnp.float32) * (1.0 / SLOTS)
        square = 0.5 * x * x
        bend = square - x * x * x * (1.0 / 3.0)
        at = jnp.where(upper, thick[j], thick[j - 1])
        mass.append(jnp.where(upper, before[j], before[j - 1]) + x * at)
        picks.append(upper)
        parts.append((at, x - square - 3.0 * bend, square - 3.0 * bend, 6.0 * bend))
    mass.append(before[LEVELS])
    layer = []
    for j in range(LEVELS):
        layer.append(mass[j + 1] - mass[j])
        outs[0][j] = layer[j]
    for field in range(5):
        part, n = ((1, 0), (1, 1), (0, 1), (2, 0), (2, 1))[field]
        f = [got[part, k, n] for k in range(LEVELS)]
        edge = [f[0], 0.5 * (f[0] + f[1])]
        for k in range(2, LEVELS - 1):
            edge.append((7.0 * (f[k - 1] + f[k]) - (f[k - 2] + f[k + 1])) * (1.0 / 12.0))
        edge += [0.5 * (f[-2] + f[-1]), f[-1]]
        running = jnp.zeros_like(f[0])
        sums = [running]
        for k in range(LEVELS):
            running = running + thick[k] * f[k]
            sums.append(running)
        last = sums[0]
        for j in range(1, LEVELS + 1):
            if j < LEVELS:
                upper = picks[j - 1]
                at, w_left, w_right, w_mid = parts[j - 1]
                left = jnp.where(upper, edge[j], edge[j - 1])
                right = jnp.where(upper, edge[j + 1], edge[j])
                mid = jnp.where(upper, f[j], f[j - 1])
                base = jnp.where(upper, sums[j], sums[j - 1])
                content = base + at * (w_left * left + w_right * right + w_mid * mid)
            else:
                content = sums[LEVELS]
            outs[field + 1][j - 1] = (content - last) / layer[j - 1]
            last = content


def remap(got, index, slot):
    vmem = pl.BlockSpec(memory_space=pltpu.VMEM)
    return pl.pallas_call(
        remap_kernel,
        out_shape=tuple(jax.ShapeDtypeStruct((LEVELS, SUB, LANES), jnp.float32) for _ in range(6)),
        in_specs=[vmem] * 3,
        out_specs=tuple([vmem] * 6),
        name="remap",
    )(got, index, slot)


def body(thickness, wind_east, wind_north, theta, tracer, wind_vertical, cross_index, cross_slot):
    fields = [
        f.reshape(2, SUB, PIECES, LANES).transpose(0, 2, 1, 3)
        for f in (thickness, wind_east, wind_north, theta, tracer, wind_vertical)
    ]
    return tuple(remap(advance(fields), cross_index, cross_slot))


def solution(mesh):
    split = P("lev", "tile", None)
    joined = P(None, "tile", "lev")
    return jax.shard_map(
        body,
        mesh=mesh,
        in_specs=(split,) * 6 + (joined,) * 2,
        out_specs=(joined,) * 6,
        check_vma=False,
    )
```

```python
import functools

import jax
import jax.numpy as jnp
from jax import lax
from jax.experimental import pallas as pl
from jax.experimental.pallas import tpu as pltpu
from jax.sharding import PartitionSpec as P

MESH = pl.DeviceIdType.MESH

COURANT = 0.1
DAMPING = 0.015
SLOPE = (45.0 / 60.0, -9.0 / 60.0, 1.0 / 60.0)
SIXTH = (15.0, -6.0, 1.0)
SLOTS = 8

LANES = 128
SUB = 8
PIECES = 8
LEVELS = 16
FIELDS = 6
PARTS = 3
COLUMNS = 16
OFF = 24
ROWS = 64
AHEAD = 2
CUTS = 1
UNROLL = 8

REACH = (((0, 16), (0, 16)), ((0, 16), (0, 16)), ((1, 15), (0, 15)), ((1, 15), (0, 15)), ((7, 9), (0, 9)), ((7, 9), (0, 9)))


def place():
    tile = lax.axis_index("tile")
    lev = lax.axis_index("lev")
    high = lax.rem(tile, 2)
    column = lax.div(tile, 2)
    ring = high * 4 + lax.div(lev, 2)
    core = lax.rem(lev, 2)
    return column, ring, core


def device(column, ring, core):
    column = lax.rem(column + 2 * COLUMNS, COLUMNS)
    ring = lax.rem(ring + 16, 8)
    return (column * 2 + lax.div(ring, 4), lax.rem(ring, 4) * 2 + core)


def owned_level(ring, core):
    first = jnp.logical_and(ring >= 2, ring < 6)
    early = 4 * (ring - 2) + 2 * core
    late = 4 * lax.rem(ring + 2, 8) + 2 * core + 1
    return jnp.where(first, early, late)


def lanes():
    return lax.broadcasted_iota(jnp.int32, (SUB, LANES), 1)


def shifted_y(get, piece, row, lane):
    before = lax.rem(piece + PIECES - 1, PIECES)
    after = lax.rem(piece + 1, PIECES)
    here, left, right = get(piece, row), get(before, row), get(after, row)
    ahead, behind = [], []
    for k in (1, 2, 3):
        ahead.append(pltpu.roll(jnp.where(lane < k, right, here), LANES - k, 1))
        behind.append(pltpu.roll(jnp.where(lane >= LANES - k, left, here), k, 1))
    return here, ahead, behind


def shifted_x(get, piece, row):
    return [get(piece, row + k) for k in (1, 2, 3)], [get(piece, row - k) for k in (1, 2, 3)]


def slope(ahead, behind):
    total = None
    for k in range(3):
        term = (-COURANT * SLOPE[k]) * (ahead[k] - behind[k])
        total = term if total is None else total + term
    return total


def weights(wind):
    plus, minus = [], []
    for k in range(3):
        carry = wind * (-COURANT * SLOPE[k])
        plus.append(DAMPING * SIXTH[k] + carry)
        minus.append(DAMPING * SIXTH[k] - carry)
    return plus, minus


def stencil(here, x_side, y_side, by_x, by_y):
    total = (1.0 - 40.0 * DAMPING) * here
    for (ahead, behind), (plus, minus) in ((x_side, by_x), (y_side, by_y)):
        for k in range(3):
            total = total + plus[k] * ahead[k]
            total = total + minus[k] * behind[k]
    return total


def reader(ref, field):
    def get(piece, row):
        return ref[field, piece, pl.ds(OFF + row, SUB), :]

    return get


def mass_piece(log_get, old, pressure, divergence, step, piece, row, lane, store, with_theta):
    east = reader(old, 1)
    north = reader(old, 2)
    by_x = weights(east(piece, row))
    n_here, n_ahead, n_behind = shifted_y(north, piece, row, lane)
    by_y = weights(n_here)
    div = slope(*shifted_x(east, piece, row)) + slope(n_ahead, n_behind)
    g_here, g_ahead, g_behind = shifted_y(log_get, piece, row, lane)
    new = stencil(g_here, shifted_x(log_get, piece, row), (g_ahead, g_behind), by_x, by_y) + div
    thick = jnp.exp(new)
    at = pl.ds(OFF + row, SUB)
    divergence[step, piece, at, :] = div
    pressure[step, piece, at, :] = reader(old, 3)(piece, row) * thick if with_theta else thick
    store(piece, row, new, thick)


def mass_stage(log_get, old, pressure, divergence, step, start, blocks, store, with_theta=True):
    def run(piece, carry):
        lane = lanes()
        for block in range(blocks):
            mass_piece(log_get, old, pressure, divergence, step, piece, start + SUB * block, lane, store, with_theta)
        return carry

    lax.fori_loop(0, PIECES, run, 0, unroll=UNROLL)


def wind_piece(old, pressure, step, piece, row, lane, with_theta=True):
    east, north, temper, press = reader(old, 1), reader(old, 2), reader(old, 3), reader(pressure, step)
    e_here, e_ahead, e_behind = shifted_y(east, piece, row, lane)
    n_here, n_ahead, n_behind = shifted_y(north, piece, row, lane)
    by_x, by_y = weights(e_here), weights(n_here)
    new_east = stencil(e_here, shifted_x(east, piece, row), (e_ahead, e_behind), by_x, by_y)
    new_east = new_east + slope(*shifted_x(press, piece, row))
    new_north = stencil(n_here, shifted_x(north, piece, row), (n_ahead, n_behind), by_x, by_y)
    _, p_ahead, p_behind = shifted_y(press, piece, row, lane)
    new_north = new_north + slope(p_ahead, p_behind)
    if not with_theta:
        return new_east, new_north
    t_here, t_ahead, t_behind = shifted_y(temper, piece, row, lane)
    new_temper = stencil(t_here, shifted_x(temper, piece, row), (t_ahead, t_behind), by_x, by_y)
    return new_east, new_north, new_temper


def theta_piece(old, piece, row, lane):
    by_x = weights(reader(old, 1)(piece, row))
    by_y = weights(reader(old, 2)(piece, row))
    get = reader(old, 3)
    here, ahead, behind = shifted_y(get, piece, row, lane)
    return stencil(here, shifted_x(get, piece, row), (ahead, behind), by_x, by_y)


def passive_piece(old, divergence, step, piece, row, lane):
    by_x = weights(reader(old, 1)(piece, row))
    by_y = weights(reader(old, 2)(piece, row))
    out = []
    for field in (4, 5):
        get = reader(old, field)
        here, ahead, behind = shifted_y(get, piece, row, lane)
        out.append(stencil(here, shifted_x(get, piece, row), (ahead, behind), by_x, by_y))
    out[1] = out[1] + divergence[step, piece, pl.ds(OFF + row, SUB), :]
    return out


def stage(body, start, blocks, store):
    def run(piece, carry):
        lane = lanes()
        for block in range(blocks):
            row = start + SUB * block
            store(piece, row, body(piece, row, lane))
        return carry

    lax.fori_loop(0, PIECES, run, 0, unroll=UNROLL)


def advance_kernel(*refs):
    inputs = refs[:FIELDS]
    got = refs[FIELDS]
    (state0, state1, state2, logs, pressure, divergence, outgoing, z_send, z_recv, x_send, x_recv, all_send, all_recv, own_sem, ready) = refs[FIELDS + 1 :]

    column, ring, core = place()
    high = lax.div(ring, 4)

    barrier = pltpu.get_barrier_semaphore()
    twin = device(column, ring, 1 - core)
    partners = [device(column + d, ring, core) for d in (2, -2, 1, -1)]
    partners += [device(column, ring + d, core) for d in (2, -2, 1, -1)] + [twin]
    for who in partners:
        pl.semaphore_signal(barrier, inc=1, device_id=who, device_id_type=MESH)
    pl.semaphore_wait(barrier, len(partners))

    half = pl.ds(pl.multiple_of(OFF + SUB * high, SUB), SUB)
    sends = []
    cut = PIECES // CUTS
    z_copies = []
    for n in range(FIELDS * CUTS):
        field, span = n // CUTS, pl.ds(n % CUTS * cut, cut)
        pair = []
        for way, (level, hop) in enumerate(((high, 2), (1 - high, -2))):
            pair.append(
                pltpu.make_async_remote_copy(
                    src_ref=inputs[field].at[level, span],
                    dst_ref=state0.at[field, span, half, :],
                    send_sem=z_send.at[n, way],
                    recv_sem=z_recv.at[n, way],
                    device_id=device(column, ring + hop, core),
                    device_id_type=MESH,
                )
            )
        z_copies.append(pair)

    for pair in z_copies[:AHEAD]:
        for copy in pair:
            copy.start()

    x_copies = [[] for _ in range(FIELDS)]

    def pass_on(n):
        field, span = n // CUTS, pl.ds(n % CUTS * cut, cut)
        if n + AHEAD < FIELDS * CUTS:
            for copy in z_copies[n]:
                copy.wait_send()
            for copy in z_copies[n + AHEAD]:
                copy.start()
        else:
            sends.extend(z_copies[n])
        for copy in z_copies[n]:
            copy.wait_recv()
        if n == 0:
            pl.semaphore_signal(ready, inc=1, device_id=twin, device_id_type=MESH)
        routes = [(way, hop, REACH[field][way], shift) for way, hop, shift in ((0, 1, -16), (1, -1, 16))]
        if field < 2:
            routes += [(2, 2, (14, 2), -32), (3, -2, (0, 2), 32)]
        for way, hop, (first, count), shift in routes:
            copy = pltpu.make_async_remote_copy(
                src_ref=state0.at[field, span, pl.ds(OFF + first, count), :],
                dst_ref=state0.at[field, span, pl.ds(OFF + first + shift, count), :],
                send_sem=x_send.at[n, way],
                recv_sem=x_recv.at[n, way],
                device_id=device(column + hop, ring, core),
                device_id_type=MESH,
            )
            copy.start()
            x_copies[field].append(copy)
            sends.append(copy)

    for n in range(4 * CUTS):
        pass_on(n)

    for copy in x_copies[0]:
        copy.wait_recv()

    def take_log(piece, carry):
        for block in range(7):
            at = pl.ds(OFF - 18 + SUB * block, SUB)
            logs[0, piece, at, :] = jnp.log(state0[0, piece, at, :])
        return carry

    lax.fori_loop(0, PIECES, take_log, 0, unroll=UNROLL)

    for field in (1, 2):
        for copy in x_copies[field]:
            copy.wait_recv()

    def keep(ref, fields):
        def store(piece, row, values):
            for field, value in zip(fields, values):
                ref[field, piece, pl.ds(OFF + row, SUB), :] = value

        return store

    def keep_log(ref):
        def store(piece, row, new, thick):
            ref[0, piece, pl.ds(OFF + row, SUB), :] = new

        return store

    def keep_thick(piece, row, new, thick):
        logs[0, piece, pl.ds(OFF + row, SUB), :] = thick

    for n in range(4 * CUTS, FIELDS * CUTS):
        pass_on(n)

    mass_stage(reader(logs, 0), state0, pressure, divergence, 0, -16, 6, keep_log(state1), with_theta=False)

    for copy in x_copies[3]:
        copy.wait_recv()

    def times_theta(piece, row, lane):
        return (pressure[0, piece, pl.ds(OFF + row, SUB), :] * reader(state0, 3)(piece, row),)

    stage(times_theta, -16, 6, keep(pressure, (0,)))
    stage(functools.partial(wind_piece, state0, pressure, 0), -12, 5, keep(state1, (1, 2, 3)))
    mass_stage(reader(state1, 0), state1, pressure, divergence, 1, -12, 5, keep_log(state2))
    stage(functools.partial(wind_piece, state1, pressure, 1), -8, 4, keep(state2, (1, 2, 3)))
    pl.semaphore_wait(ready, 1)
    level = owned_level(ring, core)
    lev = lax.rem(ring, 4) * 2 + core

    def give(piece, part, halves):
        out = outgoing.at[part]
        for tile_half in halves:
            mine = jnp.logical_and(piece == lev, high == tile_half)
            slot = piece * 2 + tile_half

            @pl.when(mine)
            def _():
                pltpu.make_async_copy(out.at[piece, tile_half], got.at[part, level], own_sem.at[part]).start()

            @pl.when(jnp.logical_not(mine))
            def _():
                pltpu.make_async_remote_copy(
                    src_ref=out.at[piece, tile_half],
                    dst_ref=got.at[part, level],
                    send_sem=all_send.at[part, slot],
                    recv_sem=all_recv.at[part, level],
                    device_id=(column * 2 + tile_half, piece),
                    device_id_type=MESH,
                ).start()

    def give_rest(part):
        def run(turn, carry):
            give(turned(turn), part, (1,))
            return carry

        lax.fori_loop(0, PIECES, run, 0)

    def turned(turn):
        return turn

    def last_mass(turn, carry):
        piece = turned(turn)
        lane = lanes()
        for block in range(3):
            mass_piece(reader(state2, 0), state2, pressure, divergence, 2, piece, -4 + SUB * block, lane, keep_thick, True)
        for tile_half in (0, 1):
            row = SUB * tile_half
            outgoing[0, piece, tile_half, 0, :, :] = logs[0, piece, pl.ds(OFF + row, SUB), :]
            outgoing[0, piece, tile_half, 1, :, :] = theta_piece(state2, piece, row, lane)
        give(piece, 0, (0,))
        return carry

    lax.fori_loop(0, PIECES, last_mass, 0, unroll=UNROLL)

    def last_winds(turn, carry):
        piece = turned(turn)
        lane = lanes()
        for tile_half in (0, 1):
            for n, value in enumerate(wind_piece(state2, pressure, 2, piece, SUB * tile_half, lane, False)):
                outgoing[1, piece, tile_half, n, :, :] = value
        give(piece, 1, (0,))
        return carry

    lax.fori_loop(0, PIECES, last_winds, 0, unroll=UNROLL)

    for field in (4, 5):
        for copy in x_copies[field]:
            copy.wait_recv()

    stage(functools.partial(passive_piece, state0, divergence, 0), -8, 4, keep(state1, (4, 5)))
    stage(functools.partial(passive_piece, state1, divergence, 1), -4, 3, keep(state2, (4, 5)))

    def last_passive(turn, carry):
        piece = turned(turn)
        lane = lanes()
        for tile_half in (0, 1):
            for n, value in enumerate(passive_piece(state2, divergence, 2, piece, SUB * tile_half, lane)):
                outgoing[2, piece, tile_half, n, :, :] = value
        give(piece, 2, (0,))
        return carry

    lax.fori_loop(0, PIECES, last_passive, 0, unroll=UNROLL)
    for part in range(PARTS):
        give_rest(part)

    for copy in sends:
        copy.wait_send()

    def sent(n, carry):
        part, slot = lax.div(n, LEVELS), lax.rem(n, LEVELS)

        @pl.when(slot != lev * 2 + high)
        def _():
            pltpu.make_async_copy(outgoing.at[0, 0, 0], outgoing.at[0, 0, 0], all_send.at[part, slot]).wait()

        return carry

    def arrived(n, carry):
        part, slot = lax.div(n, LEVELS), lax.rem(n, LEVELS)

        @pl.when(slot != level)
        def _():
            pltpu.make_async_copy(got.at[part, slot], got.at[part, slot], all_recv.at[part, slot]).wait()

        return carry

    lax.fori_loop(0, 2 * LEVELS, sent, 0)
    for part in range(PARTS):
        pltpu.make_async_copy(outgoing.at[part, 0, 0], got.at[part, 0], own_sem.at[part]).wait()
    lax.fori_loop(0, 2 * LEVELS, arrived, 0)
    lax.fori_loop(2 * LEVELS, 3 * LEVELS, sent, 0)
    lax.fori_loop(2 * LEVELS, 3 * LEVELS, arrived, 0)


def advance(fields):
    state = pltpu.VMEM((FIELDS, PIECES, ROWS, LANES), jnp.float32)
    return pl.pallas_call(
        advance_kernel,
        out_shape=jax.ShapeDtypeStruct((PARTS, LEVELS, 2, SUB, LANES), jnp.float32),
        in_specs=[pl.BlockSpec(memory_space=pl.ANY)] * FIELDS,
        out_specs=pl.BlockSpec(memory_space=pl.ANY),
        scratch_shapes=[
            state,
            state,
            state,
            pltpu.VMEM((1, PIECES, ROWS, LANES), jnp.float32),
            pltpu.VMEM((3, PIECES, ROWS, LANES), jnp.float32),
            pltpu.VMEM((3, PIECES, ROWS, LANES), jnp.float32),
            pltpu.VMEM((PARTS, PIECES, 2, 2, SUB, LANES), jnp.float32),
            pltpu.SemaphoreType.DMA((FIELDS * CUTS, 2)),
            pltpu.SemaphoreType.DMA((FIELDS * CUTS, 2)),
            pltpu.SemaphoreType.DMA((FIELDS * CUTS, 4)),
            pltpu.SemaphoreType.DMA((FIELDS * CUTS, 4)),
            pltpu.SemaphoreType.DMA((PARTS, LEVELS)),
            pltpu.SemaphoreType.DMA((PARTS, LEVELS)),
            pltpu.SemaphoreType.DMA((PARTS,)),
            pltpu.SemaphoreType.REGULAR,
        ],
        name="advance",
        compiler_params=pltpu.CompilerParams(
            collective_id=0, has_side_effects=True, vmem_limit_bytes=60 * 1024 * 1024
        ),
    )(*fields)


def remap_kernel(got, index_ref, slot_ref, *outs):
    thick = [got[0, k, 0] for k in range(LEVELS)]
    before = [jnp.zeros_like(thick[0])]
    for k in range(LEVELS):
        before.append(before[-1] + thick[k])
    picks, parts = [], []
    mass = [before[0]]
    for j in range(1, LEVELS):
        upper = index_ref[j - 1] == j
        x = slot_ref[j - 1].astype(jnp.float32) * (1.0 / SLOTS)
        square = 0.5 * x * x
        bend = square - x * x * x * (1.0 / 3.0)
        at = jnp.where(upper, thick[j], thick[j - 1])
        mass.append(jnp.where(upper, before[j], before[j - 1]) + x * at)
        picks.append(upper)
        parts.append((at, x - square - 3.0 * bend, square - 3.0 * bend, 6.0 * bend))
    mass.append(before[LEVELS])
    layer = []
    for j in range(LEVELS):
        layer.append(mass[j + 1] - mass[j])
        outs[0][j] = layer[j]
    for field in range(5):
        part, n = ((1, 0), (1, 1), (0, 1), (2, 0), (2, 1))[field]
        f = [got[part, k, n] for k in range(LEVELS)]
        edge = [f[0], 0.5 * (f[0] + f[1])]
        for k in range(2, LEVELS - 1):
            edge.append((7.0 * (f[k - 1] + f[k]) - (f[k - 2] + f[k + 1])) * (1.0 / 12.0))
        edge += [0.5 * (f[-2] + f[-1]), f[-1]]
        running = jnp.zeros_like(f[0])
        sums = [running]
        for k in range(LEVELS):
            running = running + thick[k] * f[k]
            sums.append(running)
        last = sums[0]
        for j in range(1, LEVELS + 1):
            if j < LEVELS:
                upper = picks[j - 1]
                at, w_left, w_right, w_mid = parts[j - 1]
                left = jnp.where(upper, edge[j], edge[j - 1])
                right = jnp.where(upper, edge[j + 1], edge[j])
                mid = jnp.where(upper, f[j], f[j - 1])
                base = jnp.where(upper, sums[j], sums[j - 1])
                content = base + at * (w_left * left + w_right * right + w_mid * mid)
            else:
                content = sums[LEVELS]
            outs[field + 1][j - 1] = (content - last) / layer[j - 1]
            last = content


def remap(got, index, slot):
    vmem = pl.BlockSpec(memory_space=pltpu.VMEM)
    return pl.pallas_call(
        remap_kernel,
        out_shape=tuple(jax.ShapeDtypeStruct((LEVELS, SUB, LANES), jnp.float32) for _ in range(6)),
        in_specs=[vmem] * 3,
        out_specs=tuple([vmem] * 6),
        name="remap",
    )(got, index, slot)


def body(thickness, wind_east, wind_north, theta, tracer, wind_vertical, cross_index, cross_slot):
    fields = [
        f.reshape(2, SUB, PIECES, LANES).transpose(0, 2, 1, 3)
        for f in (thickness, wind_east, wind_north, theta, tracer, wind_vertical)
    ]
    return tuple(remap(advance(fields), cross_index, cross_slot))


def solution(mesh):
    split = P("lev", "tile", None)
    joined = P(None, "tile", "lev")
    return jax.shard_map(
        body,
        mesh=mesh,
        in_specs=(split,) * 6 + (joined,) * 2,
        out_specs=(joined,) * 6,
        check_vma=False,
    )
```
